32 devices in a mesh: inp: 16 (over z, x, core), frq: 2 (over y).
Axes of the slice: x: 2, y: 2, z: 4, core: 2. Of those that a mesh axis runs over, the one named last changes fastest.
Arguments:
- voltages: bfloat16 [1024, 8, 2048], P('inp', 'frq'), may hold values from -6 to 6
- history: bfloat16 [1024, 3, 2048], P('inp'), may hold values from -6 to 6
- window: float32 [4, 2048], replicated, may hold values from -3 to 3
Outputs:
- visibilities: float32 [1024, 16, 2, 1024], P('frq', 'inp')
The draws below stay inside these ranges and needn't reach their ends.
All inputs are finite; a program needn't handle non-finite values.
Results may differ from the reference program's by a relative error of at most 0.0003.
Values may be sent and summed in bfloat16 or wider, within the bound.
A program may use at most 64 MiB of HBM per device.

```python
import math
import jax
import jax.numpy as jnp
from jax import lax

INPUTS = 1024
SAMPLES = 2048
TAPS = 4
CHANNELS = 16
FRAMES = 8
CHAN_FIRST = 504


def steps_of(own_key, shape, cuts, low, top_value):
    def one(position, shards_of):
        steps = jax.random.uniform(jax.random.fold_in(jax.random.fold_in(own_key, 6), position), (shards_of,), jnp.float32, low / len(cuts), top_value / len(cuts))
        return jnp.repeat(jnp.exp(steps), shape[position] // shards_of).reshape((-1,) + (1,) * (len(shape) - position - 1))

    factor_of = one(*cuts[0])
    for cut in cuts[1:]:
        factor_of = factor_of * one(*cut)
    return factor_of


def gaussian(own_key, dims, width, bound, shards=(), kind=jnp.bfloat16):
    entries = width * jax.random.normal(own_key, dims, jnp.float32)
    if shards:
        entries = entries * steps_of(own_key, dims, shards, -0.22, 0.18)
    return jnp.clip(entries, -bound, bound).astype(kind)


def setup_inputs(seed: int = 0) -> dict:
    key_list = jax.random.split(jax.random.key(seed), 4)
    voltages = gaussian(key_list[0], (INPUTS, FRAMES, SAMPLES), 1.0, 6.0, ((0, 16), (1, 2)))
    history = gaussian(key_list[1], (INPUTS, TAPS - 1, SAMPLES), 1.0, 6.0, ((0, 16),))
    window = gaussian(key_list[2], (TAPS, SAMPLES), TAPS ** -0.5, 3.0, (), jnp.float32)
    return dict(voltages=voltages, history=history, window=window)


def dft_table(channels, samples, first_bin):
    chan_bins = jnp.arange(channels, dtype=jnp.int32) + first_bin
    positions = jnp.arange(samples, dtype=jnp.int32)
    turns = chan_bins[:, None] * positions[None, :] % samples
    phases = turns.astype(jnp.float32) * (2.0 * math.pi / samples)
    scaling = 1.0 / math.sqrt(samples)
    return jnp.stack([jnp.cos(phases), -jnp.sin(phases)], axis=1) * scaling

def reference(voltages, history, window):
    weights = dft_table(CHANNELS, SAMPLES, CHAN_FIRST)
    block_inputs = min(INPUTS, 64)
    num_blocks = INPUTS // block_inputs

    def one_block(pair):
        volt_block, hist_block = pair
        extended = jnp.concatenate([hist_block, volt_block], axis=1).astype(jnp.float32)
        filtered = window[0] * extended[:, 0:FRAMES, :]
        for tap_index in range(1, TAPS):
            filtered = filtered + window[tap_index] * extended[:, tap_index:tap_index + FRAMES, :]
        return jnp.einsum('itn,cpn->citp', filtered, weights, precision=lax.Precision.HIGHEST)
    spectra = lax.map(one_block, (voltages.reshape(num_blocks, block_inputs, FRAMES, SAMPLES), history.reshape(num_blocks, block_inputs, TAPS - 1, SAMPLES)))
    spectra = jnp.moveaxis(spectra, 0, 1).reshape(CHANNELS, INPUTS, FRAMES, 2)

    def one_channel(chan_data):
        real_side = chan_data.transpose(1, 2, 0).reshape(2 * FRAMES, INPUTS)
        swapped = jnp.stack([chan_data[:, :, 1], -chan_data[:, :, 0]], axis=2)
        imag_side = swapped.transpose(1, 2, 0).reshape(2 * FRAMES, INPUTS)
        real_part = jnp.dot(real_side.T, real_side, precision=lax.Precision.HIGHEST)
        imag_part = jnp.dot(imag_side.T, real_side, precision=lax.Precision.HIGHEST)
        return jnp.stack([real_part, imag_part], axis=1)
    summed = lax.map(one_channel, spectra)
    return jnp.transpose(summed, (1, 0, 2, 3)) / FRAMES
```

```python
import functools
import math

import jax
import jax.numpy as jnp
import numpy as np
from jax import lax
from jax.experimental import pallas as pl
from jax.experimental.pallas import tpu as pltpu
from jax.sharding import PartitionSpec as P

CH_DEV = 1
LANES = 128
SUBL = 8
MESH = pl.DeviceIdType.MESH


def dft_rows(channels, samples):
    first_bin = (samples // 2 - channels) // 2
    bins = np.arange(channels, dtype=np.int64) + first_bin
    turns = bins[:, None] * np.arange(samples, dtype=np.int64)[None, :] % samples
    phases = turns * (2.0 * math.pi / samples)
    table = np.concatenate([np.cos(phases), -np.sin(phases)], axis=0) / math.sqrt(samples)
    return table.astype(np.float32)


def split_bf16(value, pieces):
    out = []
    for _ in range(pieces):
        piece = value.astype(jnp.bfloat16)
        out.append(piece)
        value = value - piece.astype(jnp.float32)
    return out


def spectra_kernel(
    cfg, x_hbm, h_hbm, table_hbm, window_hbm, out_ref,
    x_scr, table_scr, window_scr, mat_scr, z_scr, msg_scr, recv_scr,
    in_sem, send_sem, recv_sem,
):
    n_inp, n_frq, n_loc, frames, hpad, taps, channels = cfg
    n_dev = n_inp * n_frq
    my_inp = lax.axis_index("inp")
    my_frq = lax.axis_index("frq")
    me = my_inp * n_frq + my_frq
    v_rows = n_loc * frames
    loads = [
        pltpu.make_async_copy(table_hbm, table_scr, in_sem.at[0]),
        pltpu.make_async_copy(window_hbm, window_scr, in_sem.at[1]),
        pltpu.make_async_copy(x_hbm, x_scr.at[pl.ds(0, v_rows)], in_sem.at[2]),
        pltpu.make_async_copy(h_hbm, x_scr.at[pl.ds(v_rows, n_loc * hpad)], in_sem.at[3]),
    ]
    for load in loads:
        load.start()

    barrier = pltpu.get_barrier_semaphore()

    def greet(step, carry):
        dest = lax.rem(me + step, n_dev)
        pl.semaphore_signal(
            barrier, inc=1, device_id=(dest // n_frq, dest % n_frq), device_id_type=MESH
        )
        return carry

    lax.fori_loop(1, n_dev, greet, 0)

    loads[0].wait()
    loads[1].wait()
    group = 2 * channels
    for tap in range(taps):
        hi, lo = split_bf16(window_scr[tap : tap + 1, :] * table_scr[...], 2)
        mat_scr[tap * group : (tap + 1) * group, :] = hi
        mat_scr[(taps + tap) * group : (taps + tap + 1) * group, :] = lo
    loads[2].wait()
    loads[3].wait()
    z = lax.dot_general(
        x_scr[...], mat_scr[...], (((1,), (1,)), ((), ())), preferred_element_type=jnp.float32
    )
    half = taps * group
    tiles = half // LANES
    for tile in range(tiles):
        z_scr[tile] = (
            z[:, tile * LANES : (tile + 1) * LANES]
            + z[:, half + tile * LANES : half + (tile + 1) * LANES]
        )

    first = my_frq == 0

    def frame(tile, u):
        if u >= frames:
            return None
        if u >= 0:
            return z_scr[tile, pl.ds(u, n_loc, stride=frames), :]
        rows = z_scr[tile, pl.ds(v_rows + u + taps - 1, n_loc, stride=hpad), :]
        return jnp.where(first, rows, 0.0)

    held = {(tile, u): frame(tile, u) for tile in range(tiles) for u in range(1 - taps, frames)}
    per_tile = LANES // group
    lane_group = lax.broadcasted_iota(jnp.int32, (n_loc, LANES), 1) // group
    per_lane = LANES // n_loc
    n_q = 2 * frames // per_lane
    msg_rows = msg_scr.shape[0] // channels

    def frame_products(tile, t):
        total = jnp.zeros((n_loc, LANES), jnp.float32)
        for g in range(per_tile):
            u = t - (taps - 1) + tile * per_tile + g
            part = held.get((tile, u))
            if part is not None:
                total = jnp.where(lane_group == g, part, total)
        return total

    for q in range(n_q):
        acc = None
        for tile in range(tiles):
            block = jnp.concatenate(
                [frame_products(tile, q * per_lane + c) for c in range(per_lane)], axis=0
            ).T
            for g in range(per_tile):
                part = block[g * group : (g + 1) * group]
                acc = part if acc is None else acc + part
        for part in range(2):
            for jb in range(channels // SUBL):
                row = part * channels + jb * SUBL
                msg_scr[
                    pl.ds(jb * SUBL * msg_rows + part * n_q + q, SUBL, stride=msg_rows), :
                ] = acc[row : row + SUBL]
    if msg_rows > 2 * n_q:
        for row in range(2 * n_q, msg_rows):
            for jb in range(channels // SUBL):
                msg_scr[pl.ds(jb * SUBL * msg_rows + row, SUBL, stride=msg_rows), :] = jnp.zeros(
                    (SUBL, LANES), jnp.float32
                )

    recv_scr[pl.ds(pl.multiple_of(me * msg_rows, SUBL), msg_rows), :] = msg_scr[
        pl.ds(pl.multiple_of(my_inp * msg_rows, SUBL), msg_rows), :
    ]
    pl.semaphore_wait(barrier, n_dev - 1)

    def send(step, carry):
        dest = lax.rem(me + step, n_dev)
        to_inp = dest // n_frq
        pltpu.make_async_remote_copy(
            src_ref=msg_scr.at[pl.ds(pl.multiple_of(to_inp * msg_rows, SUBL), msg_rows)],
            dst_ref=recv_scr.at[pl.ds(pl.multiple_of(me * msg_rows, SUBL), msg_rows)],
            send_sem=send_sem,
            recv_sem=recv_sem,
            device_id=(to_inp, dest % n_frq),
            device_id_type=MESH,
        ).start()
        return carry

    lax.fori_loop(1, n_dev, send, 0)
    everything = pltpu.make_async_remote_copy(
        src_ref=recv_scr.at[pl.ds(0, (n_dev - 1) * msg_rows)],
        dst_ref=recv_scr.at[pl.ds(0, (n_dev - 1) * msg_rows)],
        send_sem=send_sem,
        recv_sem=recv_sem,
        device_id=(my_inp, my_frq),
        device_id_type=MESH,
    )
    everything.wait_recv()

    row = lax.broadcasted_iota(jnp.int32, (msg_rows, LANES), 0)
    own = (row % n_q < n_q // 2) & (row < 2 * n_q)
    later = (row % n_q >= n_q // 2) & (row < 2 * n_q)
    lane_part = lax.broadcasted_iota(jnp.int32, (msg_rows, LANES), 1) // n_loc

    for m in range(n_inp // per_lane):
        msgs = [
            [
                recv_scr[((m * per_lane + e) * n_frq + f) * msg_rows :
                         ((m * per_lane + e) * n_frq + f + 1) * msg_rows, :]
                for e in range(per_lane)
            ]
            for f in range(n_frq)
        ]
        for c in range(per_lane):
            lined = []
            for f in range(n_frq):
                tile = None
                for e in range(per_lane):
                    turn = (e - c) * n_loc % LANES
                    piece = pltpu.roll(msgs[f][e], turn, 1) if turn else msgs[f][e]
                    tile = piece if tile is None else jnp.where(lane_part == e, piece, tile)
                lined.append(tile)
            shift = n_q // 2
            for pair in range(n_frq // 2):
                even, odd = lined[2 * pair], lined[2 * pair + 1]
                total = even + jnp.where(later, pltpu.roll(odd, shift, 0), 0.0)
                if pair:
                    before = pltpu.roll(lined[2 * pair - 1], msg_rows - shift, 0)
                    total = total + jnp.where(own, before, 0.0)
                at = (pair * per_lane + c) * msg_rows
                out_ref[at : at + msg_rows, m * LANES : (m + 1) * LANES] = total
    everything.wait_send()


def gram_kernel(cfg, spec_ref, out_ref, right_scr):
    n_q, msg_rows, row_block, total_frames, rows_dev = cfg
    depth, inputs = spec_ref.shape
    step = pl.program_id(0)

    @pl.when(step == 0)
    def _():
        h, m, l = split_bf16(spec_ref[...], 3)
        right_scr[...] = jnp.concatenate([h, m, h, l, h, m], axis=0)

    start = pl.multiple_of(lax.axis_index("frq") * rows_dev + step * row_block, LANES)
    left = spec_ref[:, pl.ds(start, row_block)] * (1.0 / total_frames)
    row = lax.broadcasted_iota(jnp.int32, left.shape, 0) % msg_rows
    swapped = jnp.concatenate(
        [
            jnp.where(
                row[:msg_rows] < n_q,
                pltpu.roll(left[at : at + msg_rows], msg_rows - n_q, 0),
                -pltpu.roll(left[at : at + msg_rows], n_q, 0),
            )
            for at in range(0, depth, msg_rows)
        ],
        axis=0,
    )
    h, m, l = split_bf16(jnp.concatenate([left, swapped], axis=1), 3)
    stack = jnp.concatenate([h, h, m, h, l, m], axis=0)
    vis = lax.dot_general(
        stack, right_scr[...], (((0,), (0,)), ((), ())), preferred_element_type=jnp.float32
    )
    per_row = 2 * inputs // LANES
    for part in range(2):
        for rb in range(row_block // SUBL):
            at = part * row_block + rb * SUBL
            for tile in range(inputs // LANES):
                out_ref[pl.ds(rb * SUBL * per_row + 2 * tile + part, SUBL, stride=per_row), :] = vis[
                    at : at + SUBL, tile * LANES : (tile + 1) * LANES
                ]


def body(n_inp, n_frq, voltages, history, window):
    n_loc, frames, samples = voltages.shape
    taps = window.shape[0]
    inputs = n_loc * n_inp
    channels = CH_DEV * n_inp
    hpad = -(-(taps - 1) // 4) * 4
    x = voltages.reshape(n_loc * frames, samples)
    h = jnp.pad(history, ((0, 0), (0, hpad - (taps - 1)), (0, 0))).reshape(n_loc * hpad, samples)
    table = jnp.asarray(dft_rows(channels, samples))

    per_lane = LANES // n_loc
    n_q = 2 * frames // per_lane
    msg_rows = -(-2 * n_q // SUBL) * SUBL
    depth = (n_frq // 2) * per_lane * msg_rows
    x_rows = n_loc * (frames + hpad)
    n_dev = n_inp * n_frq
    half = taps * 2 * channels
    spectra = pl.pallas_call(
        functools.partial(
            spectra_kernel, (n_inp, n_frq, n_loc, frames, hpad, taps, channels)
        ),
        out_shape=jax.ShapeDtypeStruct((depth, inputs), jnp.float32),
        in_specs=[pl.BlockSpec(memory_space=pl.ANY)] * 4,
        out_specs=pl.BlockSpec(memory_space=pltpu.VMEM),
        scratch_shapes=[
            pltpu.VMEM((x_rows, samples), jnp.bfloat16),
            pltpu.VMEM((2 * channels, samples), jnp.float32),
            pltpu.VMEM((taps, samples), jnp.float32),
            pltpu.VMEM((2 * half, samples), jnp.bfloat16),
            pltpu.VMEM((half // LANES, x_rows, LANES), jnp.float32),
            pltpu.VMEM((channels * msg_rows, LANES), jnp.float32),
            pltpu.VMEM((n_dev * msg_rows, LANES), jnp.float32),
            pltpu.SemaphoreType.DMA((4,)),
            pltpu.SemaphoreType.DMA,
            pltpu.SemaphoreType.DMA,
        ],
        compiler_params=pltpu.CompilerParams(
            collective_id=0, has_side_effects=True, vmem_limit_bytes=32 * 2**20
        ),
        name="spectra_exchange",
    )(x, h, table, window)

    rows_dev = inputs // n_frq
    row_block = min(LANES, rows_dev)
    per_row = 2 * inputs // LANES
    vis = pl.pallas_call(
        functools.partial(
            gram_kernel, (n_q, msg_rows, row_block, frames * n_frq, rows_dev)
        ),
        grid=(rows_dev // row_block,),
        out_shape=jax.ShapeDtypeStruct((rows_dev * per_row, LANES), jnp.float32),
        in_specs=[pl.BlockSpec((depth, inputs), lambda i: (0, 0))],
        out_specs=pl.BlockSpec((row_block * per_row, LANES), lambda i: (i, 0)),
        scratch_shapes=[pltpu.VMEM((6 * depth, inputs), jnp.bfloat16)],
        compiler_params=pltpu.CompilerParams(vmem_limit_bytes=32 * 2**20),
        name="gram",
    )(spectra)
    return (
        vis.reshape(rows_dev, inputs // LANES, 2, LANES)
        .transpose(0, 2, 1, 3)
        .reshape(rows_dev, 1, 2, inputs)
    )


def solution(mesh):
    return jax.shard_map(
        functools.partial(body, mesh.shape["inp"], mesh.shape["frq"]),
        mesh=mesh,
        in_specs=(P("inp", "frq", None), P("inp", None, None), P()),
        out_specs=P("frq", "inp", None, None),
        check_vma=False,
    )
```

```python
import functools
import math

import jax
import jax.numpy as jnp
import numpy as np
from jax import lax
from jax.experimental import pallas as pl
from jax.experimental.pallas import tpu as pltpu
from jax.sharding import PartitionSpec as P

CH_DEV = 1
LANES = 128
SUBL = 8
MESH = pl.DeviceIdType.MESH


def dft_rows(channels, samples):
    first_bin = (samples // 2 - channels) // 2
    bins = np.arange(channels, dtype=np.int64) + first_bin
    turns = bins[:, None] * np.arange(samples, dtype=np.int64)[None, :] % samples
    phases = turns * (2.0 * math.pi / samples)
    table = np.concatenate([np.cos(phases), -np.sin(phases)], axis=0) / math.sqrt(samples)
    return table.astype(np.float32)


def split_bf16(value, pieces):
    out = []
    for _ in range(pieces):
        piece = value.astype(jnp.bfloat16)
        out.append(piece)
        value = value - piece.astype(jnp.float32)
    return out


def spectra_kernel(
    cfg, x_hbm, h_hbm, table_hbm, window_hbm, out_ref,
    x_scr, h_scr, table_scr, window_scr, mat_scr, z_scr, msg_scr, recv_scr,
    in_sem, send_sem, recv_sem,
):
    n_inp, n_frq, n_loc, frames, taps, channels = cfg
    n_dev = n_inp * n_frq
    my_inp = lax.axis_index("inp")
    my_frq = lax.axis_index("frq")
    me = my_inp * n_frq + my_frq
    v_rows = n_loc * frames
    loads = [
        pltpu.make_async_copy(table_hbm, table_scr, in_sem.at[0]),
        pltpu.make_async_copy(window_hbm, window_scr, in_sem.at[1]),
        pltpu.make_async_copy(h_hbm, h_scr, in_sem.at[2]),
        pltpu.make_async_copy(x_hbm, x_scr, in_sem.at[3]),
    ]
    for load in loads:
        load.start()

    barrier = pltpu.get_barrier_semaphore()

    def greet(step, carry):
        dest = lax.rem(me + step, n_dev)
        pl.semaphore_signal(
            barrier, inc=1, device_id=(dest // n_frq, dest % n_frq), device_id_type=MESH
        )
        return carry

    lax.fori_loop(1, n_dev, greet, 0)

    loads[0].wait()
    loads[1].wait()
    group = 2 * channels
    for tap in range(taps):
        hi, lo = split_bf16(window_scr[tap : tap + 1, :] * table_scr[...], 2)
        mat_scr[tap * group : (tap + 1) * group, :] = hi
        mat_scr[(taps + tap) * group : (taps + tap + 1) * group, :] = lo
    half = taps * group
    tiles = half // LANES

    def transform(rows, at):
        z = lax.dot_general(
            rows, mat_scr[...], (((1,), (1,)), ((), ())), preferred_element_type=jnp.float32
        )
        for tile in range(tiles):
            z_scr[tile, at : at + rows.shape[0]] = (
                z[:, tile * LANES : (tile + 1) * LANES]
                + z[:, half + tile * LANES : half + (tile + 1) * LANES]
            )

    loads[2].wait()
    transform(h_scr[...], v_rows)
    loads[3].wait()
    transform(x_scr[...].reshape(v_rows, x_scr.shape[2]), 0)

    first = my_frq == 0

    def frame(tile, u):
        if u >= frames:
            return None
        if u >= 0:
            return z_scr[tile, pl.ds(u, n_loc, stride=frames), :]
        at = v_rows + (u + taps - 1) * n_loc
        rows = z_scr[tile, at : at + n_loc, :]
        return jnp.where(first, rows, 0.0)

    held = {(tile, u): frame(tile, u) for tile in range(tiles) for u in range(1 - taps, frames)}
    per_tile = LANES // group
    lane_group = lax.broadcasted_iota(jnp.int32, (n_loc, LANES), 1) // group
    per_lane = LANES // n_loc
    n_q = 2 * frames // per_lane
    msg_rows = msg_scr.shape[0] // channels

    def frame_products(tile, t):
        total = jnp.zeros((n_loc, LANES), jnp.float32)
        for g in range(per_tile):
            u = t - (taps - 1) + tile * per_tile + g
            part = held.get((tile, u))
            if part is not None:
                total = jnp.where(lane_group == g, part, total)
        return total

    for q in range(n_q):
        acc = None
        for tile in range(tiles):
            block = jnp.concatenate(
                [frame_products(tile, q * per_lane + c) for c in range(per_lane)], axis=0
            ).T
            for g in range(per_tile):
                part = block[g * group : (g + 1) * group]
                acc = part if acc is None else acc + part
        for part in range(2):
            for jb in range(channels // SUBL):
                row = part * channels + jb * SUBL
                msg_scr[
                    pl.ds(jb * SUBL * msg_rows + part * n_q + q, SUBL, stride=msg_rows), :
                ] = acc[row : row + SUBL]
    if msg_rows > 2 * n_q:
        for row in range(2 * n_q, msg_rows):
            for jb in range(channels // SUBL):
                msg_scr[pl.ds(jb * SUBL * msg_rows + row, SUBL, stride=msg_rows), :] = jnp.zeros(
                    (SUBL, LANES), jnp.float32
                )

    recv_scr[pl.ds(pl.multiple_of(me * msg_rows, SUBL), msg_rows), :] = msg_scr[
        pl.ds(pl.multiple_of(my_inp * msg_rows, SUBL), msg_rows), :
    ]
    pl.semaphore_wait(barrier, n_dev - 1)

    def send(step, carry):
        dest = lax.rem(me + step, n_dev)
        to_inp = dest // n_frq
        pltpu.make_async_remote_copy(
            src_ref=msg_scr.at[pl.ds(pl.multiple_of(to_inp * msg_rows, SUBL), msg_rows)],
            dst_ref=recv_scr.at[pl.ds(pl.multiple_of(me * msg_rows, SUBL), msg_rows)],
            send_sem=send_sem,
            recv_sem=recv_sem,
            device_id=(to_inp, dest % n_frq),
            device_id_type=MESH,
        ).start()
        return carry

    lax.fori_loop(1, n_dev, send, 0)
    everything = pltpu.make_async_remote_copy(
        src_ref=recv_scr.at[pl.ds(0, (n_dev - 1) * msg_rows)],
        dst_ref=recv_scr.at[pl.ds(0, (n_dev - 1) * msg_rows)],
        send_sem=send_sem,
        recv_sem=recv_sem,
        device_id=(my_inp, my_frq),
        device_id_type=MESH,
    )
    everything.wait_recv()

    row = lax.broadcasted_iota(jnp.int32, (msg_rows, LANES), 0)
    own = (row % n_q < n_q // 2) & (row < 2 * n_q)
    later = (row % n_q >= n_q // 2) & (row < 2 * n_q)
    lane_part = lax.broadcasted_iota(jnp.int32, (msg_rows, LANES), 1) // n_loc

    for m in range(n_inp // per_lane):
        msgs = [
            [
                recv_scr[((m * per_lane + e) * n_frq + f) * msg_rows :
                         ((m * per_lane + e) * n_frq + f + 1) * msg_rows, :]
                for e in range(per_lane)
            ]
            for f in range(n_frq)
        ]
        for c in range(per_lane):
            lined = []
            for f in range(n_frq):
                tile = None
                for e in range(per_lane):
                    turn = (e - c) * n_loc % LANES
                    piece = pltpu.roll(msgs[f][e], turn, 1) if turn else msgs[f][e]
                    tile = piece if tile is None else jnp.where(lane_part == e, piece, tile)
                lined.append(tile)
            shift = n_q // 2
            for pair in range(n_frq // 2):
                even, odd = lined[2 * pair], lined[2 * pair + 1]
                total = even + jnp.where(later, pltpu.roll(odd, shift, 0), 0.0)
                if pair:
                    before = pltpu.roll(lined[2 * pair - 1], msg_rows - shift, 0)
                    total = total + jnp.where(own, before, 0.0)
                at = (pair * per_lane + c) * msg_rows
                out_ref[at : at + msg_rows, m * LANES : (m + 1) * LANES] = total
    everything.wait_send()


def gram_kernel(cfg, spec_ref, out_ref, right_scr):
    n_q, msg_rows, row_block, total_frames, rows_dev = cfg
    depth, inputs = spec_ref.shape
    step = pl.program_id(0)

    @pl.when(step == 0)
    def _():
        h, m, l = split_bf16(spec_ref[...], 3)
        right_scr[...] = jnp.concatenate([h, m, h, l, h, m], axis=0)

    start = pl.multiple_of(lax.axis_index("frq") * rows_dev + step * row_block, LANES)
    left = spec_ref[:, pl.ds(start, row_block)] * (1.0 / total_frames)
    row = lax.broadcasted_iota(jnp.int32, left.shape, 0) % msg_rows
    swapped = jnp.concatenate(
        [
            jnp.where(
                row[:msg_rows] < n_q,
                pltpu.roll(left[at : at + msg_rows], msg_rows - n_q, 0),
                -pltpu.roll(left[at : at + msg_rows], n_q, 0),
            )
            for at in range(0, depth, msg_rows)
        ],
        axis=0,
    )
    h, m, l = split_bf16(jnp.concatenate([left, swapped], axis=1), 3)
    stack = jnp.concatenate([h, h, m, h, l, m], axis=0)
    vis = lax.dot_general(
        stack, right_scr[...], (((0,), (0,)), ((), ())), preferred_element_type=jnp.float32
    )
    per_row = 2 * inputs // LANES
    for part in range(2):
        for rb in range(row_block // SUBL):
            at = part * row_block + rb * SUBL
            for tile in range(inputs // LANES):
                out_ref[pl.ds(rb * SUBL * per_row + 2 * tile + part, SUBL, stride=per_row), :] = vis[
                    at : at + SUBL, tile * LANES : (tile + 1) * LANES
                ]


def body(n_inp, n_frq, voltages, history, window):
    n_loc, frames, samples = voltages.shape
    taps = window.shape[0]
    inputs = n_loc * n_inp
    channels = CH_DEV * n_inp
    h = history.transpose(1, 0, 2).reshape((taps - 1) * n_loc, samples)
    table = jnp.asarray(dft_rows(channels, samples))

    per_lane = LANES // n_loc
    n_q = 2 * frames // per_lane
    msg_rows = -(-2 * n_q // SUBL) * SUBL
    depth = (n_frq // 2) * per_lane * msg_rows
    x_rows = n_loc * (frames + taps - 1)
    n_dev = n_inp * n_frq
    half = taps * 2 * channels
    spectra = pl.pallas_call(
        functools.partial(
            spectra_kernel, (n_inp, n_frq, n_loc, frames, taps, channels)
        ),
        out_shape=jax.ShapeDtypeStruct((depth, inputs), jnp.float32),
        in_specs=[pl.BlockSpec(memory_space=pl.ANY)] * 4,
        out_specs=pl.BlockSpec(memory_space=pltpu.VMEM),
        scratch_shapes=[
            pltpu.VMEM((n_loc, frames, samples), jnp.bfloat16),
            pltpu.VMEM(((taps - 1) * n_loc, samples), jnp.bfloat16),
            pltpu.VMEM((2 * channels, samples), jnp.float32),
            pltpu.VMEM((taps, samples), jnp.float32),
            pltpu.VMEM((2 * half, samples), jnp.bfloat16),
            pltpu.VMEM((half // LANES, x_rows, LANES), jnp.float32),
            pltpu.VMEM((channels * msg_rows, LANES), jnp.float32),
            pltpu.VMEM((n_dev * msg_rows, LANES), jnp.float32),
            pltpu.SemaphoreType.DMA((4,)),
            pltpu.SemaphoreType.DMA,
            pltpu.SemaphoreType.DMA,
        ],
        compiler_params=pltpu.CompilerParams(
            collective_id=0, has_side_effects=True, vmem_limit_bytes=60 * 2**20
        ),
        name="spectra_exchange",
    )(voltages, h, table, window)

    rows_dev = inputs // n_frq
    row_block = min(LANES, rows_dev)
    per_row = 2 * inputs // LANES
    vis = pl.pallas_call(
        functools.partial(
            gram_kernel, (n_q, msg_rows, row_block, frames * n_frq, rows_dev)
        ),
        grid=(rows_dev // row_block,),
        out_shape=jax.ShapeDtypeStruct((rows_dev * per_row, LANES), jnp.float32),
        in_specs=[pl.BlockSpec((depth, inputs), lambda i: (0, 0))],
        out_specs=pl.BlockSpec((row_block * per_row, LANES), lambda i: (i, 0)),
        scratch_shapes=[pltpu.VMEM((6 * depth, inputs), jnp.bfloat16)],
        compiler_params=pltpu.CompilerParams(vmem_limit_bytes=32 * 2**20),
        name="gram",
    )(spectra)
    return (
        vis.reshape(rows_dev, inputs // LANES, 2, LANES)
        .transpose(0, 2, 1, 3)
        .reshape(rows_dev, 1, 2, inputs)
    )


def solution(mesh):
    return jax.shard_map(
        functools.partial(body, mesh.shape["inp"], mesh.shape["frq"]),
        mesh=mesh,
        in_specs=(P("inp", "frq", None), P("inp", None, None), P()),
        out_specs=P("frq", "inp", None, None),
        check_vma=False,
    )
```

```python
import functools
import math

import jax
import jax.numpy as jnp
import numpy as np
from jax import lax
from jax.experimental import pallas as pl
from jax.experimental.pallas import tpu as pltpu
from jax.sharding import PartitionSpec as P

CH_DEV = 1
LANES = 128
SUBL = 8
MESH = pl.DeviceIdType.MESH


def dft_rows(channels, samples):
    first_bin = (samples // 2 - channels) // 2
    bins = np.arange(channels, dtype=np.int64) + first_bin
    turns = bins[:, None] * np.arange(samples, dtype=np.int64)[None, :] % samples
    phases = turns * (2.0 * math.pi / samples)
    table = np.concatenate([np.cos(phases), -np.sin(phases)], axis=0) / math.sqrt(samples)
    return table.astype(np.float32)


def split_bf16(value, pieces):
    out = []
    for _ in range(pieces):
        piece = value.astype(jnp.bfloat16)
        out.append(piece)
        value = value - piece.astype(jnp.float32)
    return out


def spectra_kernel(
    cfg, x_hbm, h_hbm, table_hbm, window_hbm, out_hbm,
    x_scr, h_scr, table_scr, window_scr, mat_scr, z_scr, msg_scr,
    in_sem, send_sem, recv_sem,
):
    n_inp, n_frq, n_loc, frames, taps, channels = cfg
    n_dev = n_inp * n_frq
    my_inp = lax.axis_index("inp")
    my_frq = lax.axis_index("frq")
    me = my_inp * n_frq + my_frq
    v_rows = n_loc * frames
    loads = [
        pltpu.make_async_copy(table_hbm, table_scr, in_sem.at[0]),
        pltpu.make_async_copy(window_hbm, window_scr, in_sem.at[1]),
        pltpu.make_async_copy(h_hbm, h_scr, in_sem.at[2]),
        pltpu.make_async_copy(x_hbm, x_scr, in_sem.at[3]),
    ]
    for load in loads:
        load.start()

    barrier = pltpu.get_barrier_semaphore()

    def greet(step, carry):
        dest = lax.rem(me + step, n_dev)
        pl.semaphore_signal(
            barrier, inc=1, device_id=(dest // n_frq, dest % n_frq), device_id_type=MESH
        )
        return carry

    lax.fori_loop(1, n_dev, greet, 0)

    loads[0].wait()
    loads[1].wait()
    group = 2 * channels
    for tap in range(taps):
        hi, lo = split_bf16(window_scr[tap : tap + 1, :] * table_scr[...], 2)
        mat_scr[tap * group : (tap + 1) * group, :] = hi
        mat_scr[(taps + tap) * group : (taps + tap + 1) * group, :] = lo
    half = taps * group
    tiles = half // LANES

    def transform(rows, at):
        z = lax.dot_general(
            rows, mat_scr[...], (((1,), (1,)), ((), ())), preferred_element_type=jnp.float32
        )
        for tile in range(tiles):
            z_scr[tile, at : at + rows.shape[0]] = (
                z[:, tile * LANES : (tile + 1) * LANES]
                + z[:, half + tile * LANES : half + (tile + 1) * LANES]
            )

    loads[2].wait()
    transform(h_scr[...], v_rows)
    loads[3].wait()
    transform(x_scr[...].reshape(v_rows, x_scr.shape[2]), 0)

    first = my_frq == 0

    def frame(tile, u):
        if u >= frames:
            return None
        if u >= 0:
            return z_scr[tile, pl.ds(u, n_loc, stride=frames), :]
        at = v_rows + (u + taps - 1) * n_loc
        rows = z_scr[tile, at : at + n_loc, :]
        return jnp.where(first, rows, 0.0)

    held = {(tile, u): frame(tile, u) for tile in range(tiles) for u in range(1 - taps, frames)}
    per_tile = LANES // group
    lane_group = lax.broadcasted_iota(jnp.int32, (n_loc, LANES), 1) // group
    per_lane = LANES // n_loc
    n_q = 2 * frames // per_lane
    msg_rows = msg_scr.shape[0] // channels

    def frame_products(tile, t):
        total = jnp.zeros((n_loc, LANES), jnp.float32)
        for g in range(per_tile):
            u = t - (taps - 1) + tile * per_tile + g
            part = held.get((tile, u))
            if part is not None:
                total = jnp.where(lane_group == g, part, total)
        return total

    for q in range(n_q):
        acc = None
        for tile in range(tiles):
            block = jnp.concatenate(
                [frame_products(tile, q * per_lane + c) for c in range(per_lane)], axis=0
            ).T
            for g in range(per_tile):
                part = block[g * group : (g + 1) * group]
                acc = part if acc is None else acc + part
        for part in range(2):
            for jb in range(channels // SUBL):
                row = part * channels + jb * SUBL
                msg_scr[
                    pl.ds(jb * SUBL * msg_rows + part * n_q + q, SUBL, stride=msg_rows), :
                ] = acc[row : row + SUBL]
    if msg_rows > 2 * n_q:
        for row in range(2 * n_q, msg_rows):
            for jb in range(channels // SUBL):
                msg_scr[pl.ds(jb * SUBL * msg_rows + row, SUBL, stride=msg_rows), :] = jnp.zeros(
                    (SUBL, LANES), jnp.float32
                )

    my_slot = out_hbm.at[pl.ds(pl.multiple_of(me * msg_rows, SUBL), msg_rows)]
    mine = pltpu.make_async_copy(
        msg_scr.at[pl.ds(pl.multiple_of(my_inp * msg_rows, SUBL), msg_rows)],
        my_slot,
        in_sem.at[4],
    )
    mine.start()
    pl.semaphore_wait(barrier, n_dev - 1)

    def send(step, carry):
        dest = lax.rem(me + step, n_dev)
        to_inp = dest // n_frq
        pltpu.make_async_remote_copy(
            src_ref=msg_scr.at[pl.ds(pl.multiple_of(to_inp * msg_rows, SUBL), msg_rows)],
            dst_ref=my_slot,
            send_sem=send_sem,
            recv_sem=recv_sem,
            device_id=(to_inp, dest % n_frq),
            device_id_type=MESH,
        ).start()
        return carry

    lax.fori_loop(1, n_dev, send, 0)
    everything = pltpu.make_async_remote_copy(
        src_ref=out_hbm.at[pl.ds(0, (n_dev - 1) * msg_rows)],
        dst_ref=out_hbm.at[pl.ds(0, (n_dev - 1) * msg_rows)],
        send_sem=send_sem,
        recv_sem=recv_sem,
        device_id=(my_inp, my_frq),
        device_id_type=MESH,
    )
    everything.wait_recv()

    mine.wait()
    everything.wait_send()


def gram_kernel(cfg, msg_hbm, out_hbm, msg_scr, spec_ref, vis_scr, in_sem, out_sem):
    n_inp, n_frq, n_loc, n_q, msg_rows, row_block, total_frames, rows_dev = cfg
    depth, inputs = spec_ref.shape
    per_lane = LANES // n_loc
    load = pltpu.make_async_copy(msg_hbm, msg_scr, in_sem)
    load.start()
    load.wait()

    row = lax.broadcasted_iota(jnp.int32, (msg_rows, LANES), 0)
    own = (row % n_q < n_q // 2) & (row < 2 * n_q)
    later = (row % n_q >= n_q // 2) & (row < 2 * n_q)
    lane_part = lax.broadcasted_iota(jnp.int32, (msg_rows, LANES), 1) // n_loc

    for m in range(n_inp // per_lane):
        msgs = [
            [
                msg_scr[((m * per_lane + e) * n_frq + f) * msg_rows :
                         ((m * per_lane + e) * n_frq + f + 1) * msg_rows, :]
                for e in range(per_lane)
            ]
            for f in range(n_frq)
        ]
        for c in range(per_lane):
            lined = []
            for f in range(n_frq):
                tile = None
                for e in range(per_lane):
                    turn = (e - c) * n_loc % LANES
                    piece = pltpu.roll(msgs[f][e], turn, 1) if turn else msgs[f][e]
                    tile = piece if tile is None else jnp.where(lane_part == e, piece, tile)
                lined.append(tile)
            shift = n_q // 2
            for pair in range(n_frq // 2):
                even, odd = lined[2 * pair], lined[2 * pair + 1]
                total = even + jnp.where(later, pltpu.roll(odd, shift, 0), 0.0)
                if pair:
                    before = pltpu.roll(lined[2 * pair - 1], msg_rows - shift, 0)
                    total = total + jnp.where(own, before, 0.0)
                at = (pair * per_lane + c) * msg_rows
                spec_ref[at : at + msg_rows, m * LANES : (m + 1) * LANES] = total

    h, m, l = split_bf16(spec_ref[...], 3)
    right = jnp.concatenate([h, m, h, l, h, m], axis=0)
    anchor = lax.axis_index("frq") * rows_dev
    copies = []
    for step in range(rows_dev // row_block):
        start = pl.multiple_of(anchor + step * row_block, LANES)
        left = spec_ref[:, pl.ds(start, row_block)] * (1.0 / total_frames)
        row = lax.broadcasted_iota(jnp.int32, left.shape, 0) % msg_rows
        swapped = jnp.concatenate(
            [
                jnp.where(
                    row[:msg_rows] < n_q,
                    pltpu.roll(left[at : at + msg_rows], msg_rows - n_q, 0),
                    -pltpu.roll(left[at : at + msg_rows], n_q, 0),
                )
                for at in range(0, depth, msg_rows)
            ],
            axis=0,
        )
        for part, side in enumerate((left, swapped)):
            h, m, l = split_bf16(side, 3)
            stack = jnp.concatenate([h, h, m, h, l, m], axis=0)
            vis = lax.dot_general(
                stack, right, (((0,), (0,)), ((), ())), preferred_element_type=jnp.float32
            )
            rows = pl.ds(step * row_block, row_block)
            for tile in range(inputs // LANES):
                at = 2 * tile + part
                vis_scr[at, rows, :] = vis[:, tile * LANES : (tile + 1) * LANES]
                copy = pltpu.make_async_copy(
                    vis_scr.at[at, rows], out_hbm.at[rows, at], out_sem.at[len(copies)]
                )
                copy.start()
                copies.append(copy)
    for copy in copies:
        copy.wait()


def body(n_inp, n_frq, voltages, history, window):
    n_loc, frames, samples = voltages.shape
    taps = window.shape[0]
    inputs = n_loc * n_inp
    channels = CH_DEV * n_inp
    h = history.transpose(1, 0, 2).reshape((taps - 1) * n_loc, samples)
    table = jnp.asarray(dft_rows(channels, samples))

    per_lane = LANES // n_loc
    n_q = 2 * frames // per_lane
    msg_rows = -(-2 * n_q // SUBL) * SUBL
    depth = (n_frq // 2) * per_lane * msg_rows
    x_rows = n_loc * (frames + taps - 1)
    n_dev = n_inp * n_frq
    half = taps * 2 * channels
    spectra = pl.pallas_call(
        functools.partial(
            spectra_kernel, (n_inp, n_frq, n_loc, frames, taps, channels)
        ),
        out_shape=jax.ShapeDtypeStruct((n_dev * msg_rows, LANES), jnp.float32),
        in_specs=[pl.BlockSpec(memory_space=pl.ANY)] * 4,
        out_specs=pl.BlockSpec(memory_space=pl.ANY),
        scratch_shapes=[
            pltpu.VMEM((n_loc, frames, samples), jnp.bfloat16),
            pltpu.VMEM(((taps - 1) * n_loc, samples), jnp.bfloat16),
            pltpu.VMEM((2 * channels, samples), jnp.float32),
            pltpu.VMEM((taps, samples), jnp.float32),
            pltpu.VMEM((2 * half, samples), jnp.bfloat16),
            pltpu.VMEM((half // LANES, x_rows, LANES), jnp.float32),
            pltpu.VMEM((channels * msg_rows, LANES), jnp.float32),
            pltpu.SemaphoreType.DMA((5,)),
            pltpu.SemaphoreType.DMA,
            pltpu.SemaphoreType.DMA,
        ],
        compiler_params=pltpu.CompilerParams(
            collective_id=0, has_side_effects=True, vmem_limit_bytes=60 * 2**20
        ),
        name="spectra_exchange",
    )(voltages, h, table, window)

    rows_dev = inputs // n_frq
    row_block = min(LANES, rows_dev)
    per_row = 2 * inputs // LANES
    vis = pl.pallas_call(
        functools.partial(
            gram_kernel,
            (n_inp, n_frq, n_loc, n_q, msg_rows, row_block, frames * n_frq, rows_dev),
        ),
        out_shape=jax.ShapeDtypeStruct((rows_dev, per_row, LANES), jnp.float32),
        in_specs=[pl.BlockSpec(memory_space=pl.ANY)],
        out_specs=pl.BlockSpec(memory_space=pl.ANY),
        scratch_shapes=[
            pltpu.VMEM((n_dev * msg_rows, LANES), jnp.float32),
            pltpu.VMEM((depth, inputs), jnp.float32),
            pltpu.VMEM((per_row, rows_dev, LANES), jnp.float32),
            pltpu.SemaphoreType.DMA,
            pltpu.SemaphoreType.DMA((rows_dev // row_block * per_row,)),
        ],
        compiler_params=pltpu.CompilerParams(vmem_limit_bytes=60 * 2**20),
        name="gram",
    )(spectra)
    return (
        vis.reshape(rows_dev, inputs // LANES, 2, LANES)
        .transpose(0, 2, 1, 3)
        .reshape(rows_dev, 1, 2, inputs)
    )


def solution(mesh):
    return jax.shard_map(
        functools.partial(body, mesh.shape["inp"], mesh.shape["frq"]),
        mesh=mesh,
        in_specs=(P("inp", "frq", None), P("inp", None, None), P()),
        out_specs=P("frq", "inp", None, None),
        check_vma=False,
    )
```

```python
import functools
import math

import jax
import jax.numpy as jnp
import numpy as np
from jax import lax
from jax.experimental import pallas as pl
from jax.experimental.pallas import tpu as pltpu
from jax.sharding import PartitionSpec as P

CH_DEV = 1
LANES = 128
SUBL = 8
MESH = pl.DeviceIdType.MESH


def dft_rows(channels, samples):
    first_bin = (samples // 2 - channels) // 2
    bins = np.arange(channels, dtype=np.int64) + first_bin
    turns = bins[:, None] * np.arange(samples, dtype=np.int64)[None, :] % samples
    phases = turns * (2.0 * math.pi / samples)
    table = np.concatenate([np.cos(phases), -np.sin(phases)], axis=0) / math.sqrt(samples)
    return table.astype(np.float32)


def split_bf16(value, pieces):
    out = []
    for _ in range(pieces):
        piece = value.astype(jnp.bfloat16)
        out.append(piece)
        value = value - piece.astype(jnp.float32)
    return out


def to_others(n_inp, n_frq, my_inp, my_frq, act):
    def group(ahead, low):
        to_inp = lax.rem(my_inp + ahead, n_inp)
        for turn in range(low, n_frq):
            act(to_inp, lax.rem(my_frq + turn, n_frq))

    if n_inp * n_frq <= 32:
        for step in range(n_inp - 1):
            group((n_inp // 2 + step) % n_inp if step < n_inp // 2 else n_inp - 1 - step, 0)
    else:
        lax.fori_loop(1, n_inp, lambda step, carry: (group(step, 0), carry)[1], 0)
    group(0, 1)


def spectra_kernel(
    cfg, x_hbm, h_hbm, table_hbm, window_hbm, out_hbm,
    x_scr, h_scr, table_scr, window_scr, mat_scr, z_scr, msg_scr,
    in_sem, send_sem, recv_sem,
):
    n_inp, n_frq, n_loc, frames, taps, channels = cfg
    n_dev = n_inp * n_frq
    my_inp = lax.axis_index("inp")
    my_frq = lax.axis_index("frq")
    me = my_inp * n_frq + my_frq
    v_rows = n_loc * frames
    loads = [
        pltpu.make_async_copy(table_hbm, table_scr, in_sem.at[0]),
        pltpu.make_async_copy(window_hbm, window_scr, in_sem.at[1]),
        pltpu.make_async_copy(h_hbm, h_scr, in_sem.at[2]),
        pltpu.make_async_copy(x_hbm, x_scr, in_sem.at[3]),
    ]
    for load in loads:
        load.start()

    barrier = pltpu.get_barrier_semaphore()

    def greet(to_inp, to_frq):
        pl.semaphore_signal(barrier, inc=1, device_id=(to_inp, to_frq), device_id_type=MESH)

    to_others(n_inp, n_frq, my_inp, my_frq, greet)

    loads[0].wait()
    loads[1].wait()
    group = 2 * channels
    for tap in range(taps):
        hi, lo = split_bf16(window_scr[tap : tap + 1, :] * table_scr[...], 2)
        mat_scr[tap * group : (tap + 1) * group, :] = hi
        mat_scr[(taps + tap) * group : (taps + tap + 1) * group, :] = lo
    half = taps * group
    tiles = half // LANES

    loads[2].wait()
    loads[3].wait()
    rows = jnp.concatenate([x_scr[...].reshape(v_rows, x_scr.shape[2]), h_scr[...]], axis=0)
    z = lax.dot_general(
        rows, mat_scr[...], (((1,), (1,)), ((), ())), preferred_element_type=jnp.float32
    )
    for tile in range(tiles):
        z_scr[tile] = (
            z[:, tile * LANES : (tile + 1) * LANES]
            + z[:, half + tile * LANES : half + (tile + 1) * LANES]
        )

    first = my_frq == 0

    def frame(tile, u):
        if u >= frames:
            return None
        if u >= 0:
            return z_scr[tile, pl.ds(u, n_loc, stride=frames), :]
        at = v_rows + (u + taps - 1) * n_loc
        rows = z_scr[tile, at : at + n_loc, :]
        return jnp.where(first, rows, 0.0)

    held = {(tile, u): frame(tile, u) for tile in range(tiles) for u in range(1 - taps, frames)}
    per_tile = LANES // group
    lane_group = lax.broadcasted_iota(jnp.int32, (n_loc, LANES), 1) // group
    per_lane = LANES // n_loc
    n_q = 2 * frames // per_lane
    msg_rows = msg_scr.shape[0] // channels

    def frame_products(tile, t):
        total = jnp.zeros((n_loc, LANES), jnp.float32)
        for g in range(per_tile):
            u = t - (taps - 1) + tile * per_tile + g
            part = held.get((tile, u))
            if part is not None:
                total = jnp.where(lane_group == g, part, total)
        return total

    for q in range(n_q):
        acc = None
        for tile in range(tiles):
            block = jnp.concatenate(
                [frame_products(tile, q * per_lane + c) for c in range(per_lane)], axis=0
            ).T
            for g in range(per_tile):
                part = block[g * group : (g + 1) * group]
                acc = part if acc is None else acc + part
        for part in range(2):
            for jb in range(channels // SUBL):
                row = part * channels + jb * SUBL
                msg_scr[
                    pl.ds(jb * SUBL * msg_rows + part * n_q + q, SUBL, stride=msg_rows), :
                ] = acc[row : row + SUBL]
    if msg_rows > 2 * n_q:
        for row in range(2 * n_q, msg_rows):
            for jb in range(channels // SUBL):
                msg_scr[pl.ds(jb * SUBL * msg_rows + row, SUBL, stride=msg_rows), :] = jnp.zeros(
                    (SUBL, LANES), jnp.float32
                )

    my_slot = out_hbm.at[pl.ds(pl.multiple_of(me * msg_rows, SUBL), msg_rows)]
    mine = pltpu.make_async_copy(
        msg_scr.at[pl.ds(pl.multiple_of(my_inp * msg_rows, SUBL), msg_rows)],
        my_slot,
        in_sem.at[4],
    )
    mine.start()
    pl.semaphore_wait(barrier, n_dev - 1)

    def send(to_inp, to_frq):
        pltpu.make_async_remote_copy(
            src_ref=msg_scr.at[pl.ds(pl.multiple_of(to_inp * msg_rows, SUBL), msg_rows)],
            dst_ref=my_slot,
            send_sem=send_sem,
            recv_sem=recv_sem,
            device_id=(to_inp, to_frq),
            device_id_type=MESH,
        ).start()

    to_others(n_inp, n_frq, my_inp, my_frq, send)
    everything = pltpu.make_async_remote_copy(
        src_ref=out_hbm.at[pl.ds(0, (n_dev - 1) * msg_rows)],
        dst_ref=out_hbm.at[pl.ds(0, (n_dev - 1) * msg_rows)],
        send_sem=send_sem,
        recv_sem=recv_sem,
        device_id=(my_inp, my_frq),
        device_id_type=MESH,
    )
    everything.wait_recv()

    mine.wait()
    everything.wait_send()


def gram_kernel(cfg, msg_hbm, out_hbm, msg_scr, spec_ref, left_scr, vis_scr, in_sem, out_sem):
    n_inp, n_frq, n_loc, n_q, msg_rows, total_frames, rows_dev = cfg
    depth, inputs = spec_ref.shape
    per_lane = LANES // n_loc
    load = pltpu.make_async_copy(msg_hbm, msg_scr, in_sem)
    load.start()
    load.wait()

    row = lax.broadcasted_iota(jnp.int32, (msg_rows, LANES), 0)
    own = (row % n_q < n_q // 2) & (row < 2 * n_q)
    later = (row % n_q >= n_q // 2) & (row < 2 * n_q)
    lane_part = lax.broadcasted_iota(jnp.int32, (msg_rows, LANES), 1) // n_loc

    for m in range(n_inp // per_lane):
        msgs = [
            [
                msg_scr[((m * per_lane + e) * n_frq + f) * msg_rows :
                         ((m * per_lane + e) * n_frq + f + 1) * msg_rows, :]
                for e in range(per_lane)
            ]
            for f in range(n_frq)
        ]
        for c in range(per_lane):
            lined = []
            for f in range(n_frq):
                tile = None
                for e in range(per_lane):
                    turn = (e - c) * n_loc % LANES
                    piece = pltpu.roll(msgs[f][e], turn, 1) if turn else msgs[f][e]
                    tile = piece if tile is None else jnp.where(lane_part == e, piece, tile)
                lined.append(tile)
            shift = n_q // 2
            for pair in range(n_frq // 2):
                even, odd = lined[2 * pair], lined[2 * pair + 1]
                total = even + jnp.where(later, pltpu.roll(odd, shift, 0), 0.0)
                if pair:
                    before = pltpu.roll(lined[2 * pair - 1], msg_rows - shift, 0)
                    total = total + jnp.where(own, before, 0.0)
                at = (pair * per_lane + c) * msg_rows
                spec_ref[at : at + msg_rows, m * LANES : (m + 1) * LANES] = total

    spectra = spec_ref[...]
    h, m, l = split_bf16(spectra, 3)
    spare = [jnp.zeros_like(h)] * (-6 % (LANES // depth) if LANES % depth == 0 else 0)
    right = jnp.concatenate([h, m, h, l, h, m] + spare, axis=0)
    anchor = pl.multiple_of(lax.axis_index("frq") * rows_dev, LANES)
    left = spec_ref[:, pl.ds(anchor, rows_dev)] * (1.0 / total_frames)
    row_at = lax.broadcasted_iota(jnp.int32, (msg_rows, rows_dev), 0)
    swapped = jnp.concatenate(
        [
            jnp.where(
                row_at < n_q,
                pltpu.roll(left[at : at + msg_rows], msg_rows - n_q, 0),
                -pltpu.roll(left[at : at + msg_rows], n_q, 0),
            )
            for at in range(0, depth, msg_rows)
        ],
        axis=0,
    )
    h, m, l = split_bf16(jnp.concatenate([left, swapped], axis=1), 3)
    left_scr[...] = jnp.concatenate([h, h, m, h, l, m] + spare, axis=0).T
    width = 2 * LANES
    copies = []
    for block in range(inputs // width):
        vis = jnp.dot(
            left_scr[...],
            right[:, block * width : (block + 1) * width],
            preferred_element_type=jnp.float32,
        )
        for tile in range(2):
            for part in range(2):
                at = 2 * (2 * block + tile) + part
                vis_scr[at] = vis[
                    part * rows_dev : (part + 1) * rows_dev, tile * LANES : (tile + 1) * LANES
                ]
                copy = pltpu.make_async_copy(vis_scr.at[at], out_hbm.at[:, at], out_sem.at[at])
                copy.start()
                copies.append(copy)
    for copy in copies:
        copy.wait()


def body(n_inp, n_frq, voltages, history, window):
    n_loc, frames, samples = voltages.shape
    taps = window.shape[0]
    inputs = n_loc * n_inp
    channels = CH_DEV * n_inp
    h = history.transpose(1, 0, 2).reshape((taps - 1) * n_loc, samples)
    table = jnp.asarray(dft_rows(channels, samples))

    per_lane = LANES // n_loc
    n_q = 2 * frames // per_lane
    msg_rows = -(-2 * n_q // SUBL) * SUBL
    depth = (n_frq // 2) * per_lane * msg_rows
    x_rows = n_loc * (frames + taps - 1)
    n_dev = n_inp * n_frq
    half = taps * 2 * channels
    spectra = pl.pallas_call(
        functools.partial(
            spectra_kernel, (n_inp, n_frq, n_loc, frames, taps, channels)
        ),
        out_shape=jax.ShapeDtypeStruct((n_dev * msg_rows, LANES), jnp.float32),
        in_specs=[pl.BlockSpec(memory_space=pl.ANY)] * 4,
        out_specs=pl.BlockSpec(memory_space=pl.ANY),
        scratch_shapes=[
            pltpu.VMEM((n_loc, frames, samples), jnp.bfloat16),
            pltpu.VMEM(((taps - 1) * n_loc, samples), jnp.bfloat16),
            pltpu.VMEM((2 * channels, samples), jnp.float32),
            pltpu.VMEM((taps, samples), jnp.float32),
            pltpu.VMEM((2 * half, samples), jnp.bfloat16),
            pltpu.VMEM((half // LANES, x_rows, LANES), jnp.float32),
            pltpu.VMEM((channels * msg_rows, LANES), jnp.float32),
            pltpu.SemaphoreType.DMA((5,)),
            pltpu.SemaphoreType.DMA,
            pltpu.SemaphoreType.DMA,
        ],
        compiler_params=pltpu.CompilerParams(
            collective_id=0, has_side_effects=True, vmem_limit_bytes=60 * 2**20
        ),
        name="spectra_exchange",
    )(voltages, h, table, window)

    rows_dev = inputs // n_frq
    stack = 6 * depth if LANES % depth else -(-6 * depth // LANES) * LANES
    per_row = 2 * inputs // LANES
    vis = pl.pallas_call(
        functools.partial(
            gram_kernel,
            (n_inp, n_frq, n_loc, n_q, msg_rows, frames * n_frq, rows_dev),
        ),
        out_shape=jax.ShapeDtypeStruct((rows_dev, per_row, LANES), jnp.float32),
        in_specs=[pl.BlockSpec(memory_space=pl.ANY)],
        out_specs=pl.BlockSpec(memory_space=pl.ANY),
        scratch_shapes=[
            pltpu.VMEM((n_dev * msg_rows, LANES), jnp.float32),
            pltpu.VMEM((depth, inputs), jnp.float32),
            pltpu.VMEM((2 * rows_dev, stack), jnp.bfloat16),
            pltpu.VMEM((per_row, rows_dev, LANES), jnp.float32),
            pltpu.SemaphoreType.DMA,
            pltpu.SemaphoreType.DMA((per_row,)),
        ],
        compiler_params=pltpu.CompilerParams(vmem_limit_bytes=60 * 2**20),
        name="gram",
    )(spectra)
    return (
        vis.reshape(rows_dev, inputs // LANES, 2, LANES)
        .transpose(0, 2, 1, 3)
        .reshape(rows_dev, 1, 2, inputs)
    )


def solution(mesh):
    return jax.shard_map(
        functools.partial(body, mesh.shape["inp"], mesh.shape["frq"]),
        mesh=mesh,
        in_specs=(P("inp", "frq", None), P("inp", None, None), P()),
        out_specs=P("frq", "inp", None, None),
        check_vma=False,
    )
```

```python
import functools
import math

import jax
import jax.numpy as jnp
import numpy as np
from jax import lax
from jax.experimental import pallas as pl
from jax.experimental.pallas import tpu as pltpu
from jax.sharding import PartitionSpec as P

CH_DEV = 1
LANES = 128
SUBL = 8
MESH = pl.DeviceIdType.MESH


def dft_rows(channels, samples):
    first_bin = (samples // 2 - channels) // 2
    bins = np.arange(channels, dtype=np.int64) + first_bin
    turns = bins[:, None] * np.arange(samples, dtype=np.int64)[None, :] % samples
    phases = turns * (2.0 * math.pi / samples)
    table = np.concatenate([np.cos(phases), -np.sin(phases)], axis=0) / math.sqrt(samples)
    return table.astype(np.float32)


def split_bf16(value, pieces):
    out = []
    for _ in range(pieces):
        piece = value.astype(jnp.bfloat16)
        out.append(piece)
        value = value - piece.astype(jnp.float32)
    return out


def to_others(n_inp, n_frq, my_inp, my_frq, act):
    def group(ahead, low):
        to_inp = lax.rem(my_inp + ahead, n_inp)
        for turn in range(low, n_frq):
            act(to_inp, lax.rem(my_frq + turn, n_frq))

    if n_inp * n_frq <= 32:
        for step in range(n_inp - 1):
            group((n_inp // 2 + step) % n_inp if step < n_inp // 2 else n_inp - 1 - step, 0)
    else:
        lax.fori_loop(1, n_inp, lambda step, carry: (group(step, 0), carry)[1], 0)
    group(0, 1)


def spectra_kernel(
    cfg, x_hbm, h_hbm, table_hbm, window_hbm, out_hbm,
    x_scr, h_scr, table_scr, window_scr, mat_scr, z_scr, msg_scr,
    in_sem, send_sem, recv_sem,
):
    n_inp, n_frq, n_loc, frames, taps, channels = cfg
    n_dev = n_inp * n_frq
    my_inp = lax.axis_index("inp")
    my_frq = lax.axis_index("frq")
    me = my_inp * n_frq + my_frq
    v_rows = n_loc * frames
    loads = [
        pltpu.make_async_copy(table_hbm, table_scr, in_sem.at[0]),
        pltpu.make_async_copy(window_hbm, window_scr, in_sem.at[1]),
        pltpu.make_async_copy(h_hbm, h_scr, in_sem.at[2]),
        pltpu.make_async_copy(x_hbm, x_scr, in_sem.at[3]),
    ]
    for load in loads:
        load.start()

    barrier = pltpu.get_barrier_semaphore()

    def greet(to_inp, to_frq):
        pl.semaphore_signal(barrier, inc=1, device_id=(to_inp, to_frq), device_id_type=MESH)

    to_others(n_inp, n_frq, my_inp, my_frq, greet)

    loads[0].wait()
    loads[1].wait()
    group = 2 * channels
    for tap in range(taps):
        hi, lo = split_bf16(window_scr[tap : tap + 1, :] * table_scr[...], 2)
        mat_scr[tap * group : (tap + 1) * group, :] = hi
        mat_scr[(taps + tap) * group : (taps + tap + 1) * group, :] = lo
    half = taps * group
    tiles = half // LANES

    loads[2].wait()
    loads[3].wait()
    rows = jnp.concatenate([x_scr[...].reshape(v_rows, x_scr.shape[2]), h_scr[...]], axis=0)
    z = lax.dot_general(
        rows, mat_scr[...], (((1,), (1,)), ((), ())), preferred_element_type=jnp.float32
    )
    for tile in range(tiles):
        z_scr[tile] = (
            z[:, tile * LANES : (tile + 1) * LANES]
            + z[:, half + tile * LANES : half + (tile + 1) * LANES]
        )

    first = my_frq == 0

    def frame(tile, u):
        if u >= frames:
            return None
        if u >= 0:
            return z_scr[tile, pl.ds(u, n_loc, stride=frames), :]
        at = v_rows + (u + taps - 1) * n_loc
        rows = z_scr[tile, at : at + n_loc, :]
        return jnp.where(first, rows, 0.0)

    held = {(tile, u): frame(tile, u) for tile in range(tiles) for u in range(1 - taps, frames)}
    per_tile = LANES // group
    lane_group = lax.broadcasted_iota(jnp.int32, (n_loc, LANES), 1) // group
    per_lane = LANES // n_loc
    n_q = 2 * frames // per_lane
    half_q = n_q // 2
    msg_rows = msg_scr.shape[0] // channels

    def frame_products(tile, t):
        total = jnp.zeros((n_loc, LANES), jnp.float32)
        for g in range(per_tile):
            u = t - (taps - 1) + tile * per_tile + g
            part = held.get((tile, u))
            if part is not None:
                total = jnp.where(lane_group == g, part, total)
        return total

    for q in range(n_q):
        acc = None
        for tile in range(tiles):
            block = jnp.concatenate(
                [frame_products(tile, q * per_lane + c) for c in range(per_lane)], axis=0
            ).T
            for g in range(per_tile):
                part = block[g * group : (g + 1) * group]
                acc = part if acc is None else acc + part
        for part in range(2):
            for jb in range(channels // SUBL):
                row = part * channels + jb * SUBL
                at = q // half_q * n_q + part * half_q + q % half_q
                msg_scr[pl.ds(jb * SUBL * msg_rows + at, SUBL, stride=msg_rows), :] = acc[
                    row : row + SUBL
                ]
    if msg_rows > 2 * n_q:
        for row in range(2 * n_q, msg_rows):
            for jb in range(channels // SUBL):
                msg_scr[pl.ds(jb * SUBL * msg_rows + row, SUBL, stride=msg_rows), :] = jnp.zeros(
                    (SUBL, LANES), jnp.float32
                )

    own_rows = n_q if n_q % 4 == 0 else msg_rows

    def exchange(rows, waited):
        my_slot = out_hbm.at[pl.ds(pl.multiple_of(me * msg_rows, SUBL), rows)]

        def message(to_inp):
            return msg_scr.at[pl.ds(pl.multiple_of(to_inp * msg_rows, SUBL), rows)]

        def send(to_inp, to_frq):
            pltpu.make_async_remote_copy(
                src_ref=message(to_inp),
                dst_ref=my_slot,
                send_sem=send_sem,
                recv_sem=recv_sem,
                device_id=(to_inp, to_frq),
                device_id_type=MESH,
            ).start()

        def bytes_of(count):
            return pltpu.make_async_remote_copy(
                src_ref=out_hbm.at[pl.ds(0, count)],
                dst_ref=out_hbm.at[pl.ds(0, count)],
                send_sem=send_sem,
                recv_sem=recv_sem,
                device_id=(my_inp, my_frq),
                device_id_type=MESH,
            )

        mine = pltpu.make_async_copy(message(my_inp), my_slot, in_sem.at[4])
        mine.start()
        to_others(n_inp, n_frq, my_inp, my_frq, send)
        bytes_of(waited).wait_recv()
        bytes_of((n_dev - 1) * rows).wait_send()
        mine.wait()

    pl.semaphore_wait(barrier, n_dev - 1)
    arriving = n_inp * ((n_frq - 1) * msg_rows + own_rows)
    last = my_frq == n_frq - 1
    pl.when(last)(lambda: exchange(own_rows, arriving - own_rows))
    pl.when(jnp.logical_not(last))(lambda: exchange(msg_rows, arriving - msg_rows))


def gram_kernel(
    cfg, msg_hbm, out_hbm, msg_scr, spec_ref, left_scr, right_scr, vis_scr,
    in_sem, out_sem,
):
    n_inp, n_frq, n_loc, n_q, msg_rows, total_frames, rows_dev = cfg
    depth, inputs = spec_ref.shape
    per_lane = LANES // n_loc
    load = pltpu.make_async_copy(msg_hbm, msg_scr, in_sem)
    load.start()
    load.wait()

    row = lax.broadcasted_iota(jnp.int32, (msg_rows, LANES), 0)
    own = row < n_q
    later = (row >= n_q) & (row < 2 * n_q)
    lane_part = lax.broadcasted_iota(jnp.int32, (msg_rows, LANES), 1) // n_loc

    for m in range(n_inp // per_lane):
        msgs = [
            [
                msg_scr[((m * per_lane + e) * n_frq + f) * msg_rows :
                         ((m * per_lane + e) * n_frq + f + 1) * msg_rows, :]
                for e in range(per_lane)
            ]
            for f in range(n_frq)
        ]
        for c in range(per_lane):
            lined = []
            for f in range(n_frq):
                tile = None
                for e in range(per_lane):
                    turn = (e - c) * n_loc % LANES
                    piece = pltpu.roll(msgs[f][e], turn, 1) if turn else msgs[f][e]
                    tile = piece if tile is None else jnp.where(lane_part == e, piece, tile)
                lined.append(tile)
            for pair in range(n_frq // 2):
                even, odd = lined[2 * pair], lined[2 * pair + 1]
                total = even + jnp.where(later, pltpu.roll(odd, n_q, 0), 0.0)
                if pair:
                    before = pltpu.roll(lined[2 * pair - 1], msg_rows - n_q, 0)
                    total = total + jnp.where(own, before, 0.0)
                at = (pair * per_lane + c) * msg_rows
                spec_ref[at : at + msg_rows, m * LANES : (m + 1) * LANES] = total

    spectra = spec_ref[...]
    h, m, l = split_bf16(spectra, 3)
    spare = [jnp.zeros_like(h)] * (-6 % (LANES // depth) if LANES % depth == 0 else 0)
    right = jnp.concatenate([h, m, h, l, h, m] + spare, axis=0)
    anchor = pl.multiple_of(lax.axis_index("frq") * rows_dev, LANES)
    left = spec_ref[:, pl.ds(anchor, rows_dev)] * (1.0 / total_frames)
    row_at = lax.broadcasted_iota(jnp.int32, (msg_rows, rows_dev), 0)
    swapped = jnp.concatenate(
        [
            jnp.where(
                row_at % n_q < n_q // 2,
                pltpu.roll(left[at : at + msg_rows], msg_rows - n_q // 2, 0),
                -pltpu.roll(left[at : at + msg_rows], n_q // 2, 0),
            )
            for at in range(0, depth, msg_rows)
        ],
        axis=0,
    )
    h, m, l = split_bf16(jnp.concatenate([left, swapped], axis=1), 3)
    left_scr[...] = jnp.concatenate([h, h, m, h, l, m] + spare, axis=0).T
    right_scr[...] = right
    per_row = 2 * inputs // LANES
    block = SUBL * SUBL
    blocks = rows_dev // block

    def out_copy(step):
        rows = pl.ds(pl.multiple_of(step * block * per_row, block * per_row), block * per_row)
        return pltpu.make_async_copy(vis_scr.at[rows], out_hbm.at[rows], out_sem.at[step])

    def one_block(step, carry):
        row = pl.multiple_of(step * block, block)
        sides = [left_scr[pl.ds(part * rows_dev + row, block), :] for part in range(2)]
        vis = jnp.dot(
            jnp.concatenate(sides, axis=0), right_scr[...], preferred_element_type=jnp.float32
        )
        for part in range(2):
            for r in range(0, block, SUBL):
                for tile in range(inputs // LANES):
                    at = (row + r) * per_row + 2 * tile + part
                    vis_scr[pl.ds(at, SUBL, stride=per_row), :] = vis[
                        part * block + r : part * block + r + SUBL,
                        tile * LANES : (tile + 1) * LANES,
                    ]
        out_copy(step).start()
        return carry

    lax.fori_loop(0, blocks, one_block, 0)
    for step in range(blocks):
        out_copy(step).wait()


def body(n_inp, n_frq, voltages, history, window):
    n_loc, frames, samples = voltages.shape
    taps = window.shape[0]
    inputs = n_loc * n_inp
    channels = CH_DEV * n_inp
    h = history.transpose(1, 0, 2).reshape((taps - 1) * n_loc, samples)
    table = jnp.asarray(dft_rows(channels, samples))

    per_lane = LANES // n_loc
    n_q = 2 * frames // per_lane
    msg_rows = -(-2 * n_q // SUBL) * SUBL
    depth = (n_frq // 2) * per_lane * msg_rows
    x_rows = n_loc * (frames + taps - 1)
    n_dev = n_inp * n_frq
    half = taps * 2 * channels
    spectra = pl.pallas_call(
        functools.partial(
            spectra_kernel, (n_inp, n_frq, n_loc, frames, taps, channels)
        ),
        out_shape=jax.ShapeDtypeStruct((n_dev * msg_rows, LANES), jnp.float32),
        in_specs=[pl.BlockSpec(memory_space=pl.ANY)] * 4,
        out_specs=pl.BlockSpec(memory_space=pl.ANY),
        scratch_shapes=[
            pltpu.VMEM((n_loc, frames, samples), jnp.bfloat16),
            pltpu.VMEM(((taps - 1) * n_loc, samples), jnp.bfloat16),
            pltpu.VMEM((2 * channels, samples), jnp.float32),
            pltpu.VMEM((taps, samples), jnp.float32),
            pltpu.VMEM((2 * half, samples), jnp.bfloat16),
            pltpu.VMEM((half // LANES, x_rows, LANES), jnp.float32),
            pltpu.VMEM((channels * msg_rows, LANES), jnp.float32),
            pltpu.SemaphoreType.DMA((5,)),
            pltpu.SemaphoreType.DMA,
            pltpu.SemaphoreType.DMA,
        ],
        compiler_params=pltpu.CompilerParams(
            collective_id=0, has_side_effects=True, vmem_limit_bytes=60 * 2**20
        ),
        name="spectra_exchange",
    )(voltages, h, table, window)

    rows_dev = inputs // n_frq
    stack = 6 * depth if LANES % depth else -(-6 * depth // LANES) * LANES
    per_row = 2 * inputs // LANES
    vis = pl.pallas_call(
        functools.partial(
            gram_kernel,
            (n_inp, n_frq, n_loc, n_q, msg_rows, frames * n_frq, rows_dev),
        ),
        out_shape=jax.ShapeDtypeStruct((rows_dev * per_row, LANES), jnp.float32),
        in_specs=[pl.BlockSpec(memory_space=pl.ANY)],
        out_specs=pl.BlockSpec(memory_space=pl.ANY),
        scratch_shapes=[
            pltpu.VMEM((n_dev * msg_rows, LANES), jnp.float32),
            pltpu.VMEM((depth, inputs), jnp.float32),
            pltpu.VMEM((2 * rows_dev, stack), jnp.bfloat16),
            pltpu.VMEM((stack, inputs), jnp.bfloat16),
            pltpu.VMEM((rows_dev * per_row, LANES), jnp.float32),
            pltpu.SemaphoreType.DMA,
            pltpu.SemaphoreType.DMA((rows_dev // (SUBL * SUBL),)),
        ],
        compiler_params=pltpu.CompilerParams(vmem_limit_bytes=60 * 2**20),
        name="gram",
    )(spectra)
    return (
        vis.reshape(rows_dev, inputs // LANES, 2, LANES)
        .transpose(0, 2, 1, 3)
        .reshape(rows_dev, 1, 2, inputs)
    )


def solution(mesh):
    return jax.shard_map(
        functools.partial(body, mesh.shape["inp"], mesh.shape["frq"]),
        mesh=mesh,
        in_specs=(P("inp", "frq", None), P("inp", None, None), P()),
        out_specs=P("frq", "inp", None, None),
        check_vma=False,
    )
```

```python
import functools
import math

import jax
import jax.numpy as jnp
import numpy as np
from jax import lax
from jax.experimental import pallas as pl
from jax.experimental.pallas import tpu as pltpu
from jax.sharding import PartitionSpec as P

CH_DEV = 1
LANES = 128
SUBL = 8
MESH = pl.DeviceIdType.MESH


def dft_rows(channels, samples):
    first_bin = (samples // 2 - channels) // 2
    bins = np.arange(channels, dtype=np.int64) + first_bin
    turns = bins[:, None] * np.arange(samples, dtype=np.int64)[None, :] % samples
    phases = turns * (2.0 * math.pi / samples)
    table = np.concatenate([np.cos(phases), -np.sin(phases)], axis=0) / math.sqrt(samples)
    return table.astype(np.float32)


def split_bf16(value, pieces):
    out = []
    for _ in range(pieces):
        piece = value.astype(jnp.bfloat16)
        out.append(piece)
        value = value - piece.astype(jnp.float32)
    return out


def spectra_kernel(
    cfg, x_hbm, h_hbm, table_hbm, window_hbm, out_hbm,
    x_scr, h_scr, table_scr, window_scr, mat_scr, z_scr, msg_scr, group_scr, tile_scr,
    in_sem, near_send, near_recv, send_sem, recv_sem,
):
    n_inp, n_frq, n_loc, frames, taps, channels = cfg
    my_inp = lax.axis_index("inp")
    my_frq = lax.axis_index("frq")
    per_lane = LANES // n_loc
    members = per_lane * n_frq
    share = channels // members
    member = lax.rem(my_inp, per_lane) * n_frq + my_frq
    my_group = my_inp // per_lane
    owner = my_inp // (CH_DEV * share)
    owns_mine = owner == member
    v_rows = n_loc * frames
    loads = [
        pltpu.make_async_copy(table_hbm, table_scr, in_sem.at[0]),
        pltpu.make_async_copy(window_hbm, window_scr, in_sem.at[1]),
        pltpu.make_async_copy(h_hbm, h_scr, in_sem.at[2]),
        pltpu.make_async_copy(x_hbm, x_scr, in_sem.at[3]),
    ]
    for load in loads:
        load.start()

    barrier = pltpu.get_barrier_semaphore()

    def greet(to_inp, to_frq):
        pl.semaphore_signal(barrier, inc=1, device_id=(to_inp, to_frq), device_id_type=MESH)

    def at_member(index):
        return my_group * per_lane + index // n_frq, lax.rem(index, n_frq)

    for turn in range(1, members):
        greet(*at_member(lax.rem(member + turn, members)))
    n_groups = n_inp // per_lane
    for turn in range(n_groups):
        group_at = lax.rem(my_group + turn, n_groups)
        sender = (group_at * per_lane + owner // n_frq, lax.rem(owner, n_frq))
        if turn:
            greet(*sender)
        else:
            pl.when(jnp.logical_not(owns_mine))(functools.partial(greet, *sender))

    loads[0].wait()
    loads[1].wait()
    group = 2 * channels
    for tap in range(taps):
        hi, lo = split_bf16(window_scr[tap : tap + 1, :] * table_scr[...], 2)
        mat_scr[tap * group : (tap + 1) * group, :] = hi
        mat_scr[(taps + tap) * group : (taps + tap + 1) * group, :] = lo
    half = taps * group
    tiles = half // LANES

    loads[2].wait()
    loads[3].wait()
    rows = jnp.concatenate([x_scr[...].reshape(v_rows, x_scr.shape[2]), h_scr[...]], axis=0)
    z = lax.dot_general(
        rows, mat_scr[...], (((1,), (1,)), ((), ())), preferred_element_type=jnp.float32
    )
    for tile in range(tiles):
        z_scr[tile] = (
            z[:, tile * LANES : (tile + 1) * LANES]
            + z[:, half + tile * LANES : half + (tile + 1) * LANES]
        )

    first = my_frq == 0

    def frame(tile, u):
        if u >= frames:
            return None
        if u >= 0:
            return z_scr[tile, pl.ds(u, n_loc, stride=frames), :]
        at = v_rows + (u + taps - 1) * n_loc
        rows = z_scr[tile, at : at + n_loc, :]
        return jnp.where(first, rows, 0.0)

    held = {(tile, u): frame(tile, u) for tile in range(tiles) for u in range(1 - taps, frames)}
    per_tile = LANES // group
    lane_group = lax.broadcasted_iota(jnp.int32, (n_loc, LANES), 1) // group
    n_q = 2 * frames // per_lane
    half_q = n_q // 2
    msg_rows = msg_scr.shape[0] // channels

    def frame_products(tile, t):
        total = jnp.zeros((n_loc, LANES), jnp.float32)
        for g in range(per_tile):
            u = t - (taps - 1) + tile * per_tile + g
            part = held.get((tile, u))
            if part is not None:
                total = jnp.where(lane_group == g, part, total)
        return total

    for q in range(n_q):
        acc = None
        for tile in range(tiles):
            block = jnp.concatenate(
                [frame_products(tile, q * per_lane + c) for c in range(per_lane)], axis=0
            ).T
            for g in range(per_tile):
                part = block[g * group : (g + 1) * group]
                acc = part if acc is None else acc + part
        for part in range(2):
            for jb in range(channels // SUBL):
                row = part * channels + jb * SUBL
                at = q // half_q * n_q + part * half_q + q % half_q
                msg_scr[pl.ds(jb * SUBL * msg_rows + at, SUBL, stride=msg_rows), :] = acc[
                    row : row + SUBL
                ]
    if msg_rows > 2 * n_q:
        for row in range(2 * n_q, msg_rows):
            for jb in range(channels // SUBL):
                msg_scr[pl.ds(jb * SUBL * msg_rows + row, SUBL, stride=msg_rows), :] = jnp.zeros(
                    (SUBL, LANES), jnp.float32
                )

    greeted = members - 1 + share * n_frq - owns_mine.astype(jnp.int32)
    pl.semaphore_wait(barrier, greeted)

    def wait_for(ref, rows, sends, receives):
        return pltpu.make_async_remote_copy(
            src_ref=ref.at[pl.ds(0, rows)],
            dst_ref=ref.at[pl.ds(0, rows)],
            send_sem=sends,
            recv_sem=receives,
            device_id=(my_inp, my_frq),
            device_id_type=MESH,
        )

    span = share * msg_rows
    mine = group_scr.at[pl.ds(pl.multiple_of(member * span, SUBL), span)]
    for turn in range(1, members):
        index = lax.rem(member + turn, members)
        pltpu.make_async_remote_copy(
            src_ref=msg_scr.at[pl.ds(pl.multiple_of(index * span, SUBL), span)],
            dst_ref=mine,
            send_sem=near_send,
            recv_sem=near_recv,
            device_id=at_member(index),
            device_id_type=MESH,
        ).start()
    group_scr[pl.ds(pl.multiple_of(member * span, SUBL), span), :] = msg_scr[
        pl.ds(pl.multiple_of(member * span, SUBL), span), :
    ]
    near = wait_for(group_scr, (members - 1) * span, near_send, near_recv)
    near.wait_recv()

    row = lax.broadcasted_iota(jnp.int32, (msg_rows, LANES), 0)
    own = row < n_q
    later = (row >= n_q) & (row < 2 * n_q)
    lane_part = lax.broadcasted_iota(jnp.int32, (msg_rows, LANES), 1) // n_loc
    depth = (n_frq // 2) * per_lane * msg_rows
    my_slot = out_hbm.at[pl.ds(pl.multiple_of(my_group * depth, SUBL), depth)]
    for ch in range(share):
        for c in range(per_lane):
            lined = []
            for f in range(n_frq):
                tile = None
                for e in range(per_lane):
                    at = (e * n_frq + f) * span + ch * msg_rows
                    piece = group_scr[at : at + msg_rows, :]
                    turn = (e - c) * n_loc % LANES
                    piece = pltpu.roll(piece, turn, 1) if turn else piece
                    tile = piece if tile is None else jnp.where(lane_part == e, piece, tile)
                lined.append(tile)
            for pair in range(n_frq // 2):
                even, odd = lined[2 * pair], lined[2 * pair + 1]
                total = even + jnp.where(later, pltpu.roll(odd, n_q, 0), 0.0)
                if pair:
                    before = pltpu.roll(lined[2 * pair - 1], msg_rows - n_q, 0)
                    total = total + jnp.where(own, before, 0.0)
                at = ch * depth + (pair * per_lane + c) * msg_rows
                tile_scr[at : at + msg_rows, :] = total

    def keep(ch):
        pltpu.make_async_copy(
            tile_scr.at[pl.ds(ch * depth, depth)], my_slot, in_sem.at[4]
        ).start()

    def send(ch, to_inp, to_frq):
        pltpu.make_async_remote_copy(
            src_ref=tile_scr.at[pl.ds(ch * depth, depth)],
            dst_ref=my_slot,
            send_sem=send_sem,
            recv_sem=recv_sem,
            device_id=(to_inp, to_frq),
            device_id_type=MESH,
        ).start()

    for turn in range(n_frq - 1, -1, -1):
        for ch in range(share):
            to_inp = member * share + ch
            to = functools.partial(send, ch, to_inp, lax.rem(my_frq + turn, n_frq))
            if turn:
                to()
            else:
                pl.when(to_inp != my_inp)(to)
                pl.when(to_inp == my_inp)(functools.partial(keep, ch))
    near.wait_send()

    def finish(kept):
        if kept:
            pltpu.make_async_copy(
                tile_scr.at[pl.ds(0, depth)], my_slot, in_sem.at[4]
            ).wait()
        wait_for(out_hbm, (n_groups - kept) * depth, send_sem, recv_sem).wait_recv()
        wait_for(out_hbm, (share * n_frq - kept) * depth, send_sem, recv_sem).wait_send()

    pl.when(owns_mine)(lambda: finish(1))
    pl.when(jnp.logical_not(owns_mine))(lambda: finish(0))


def gram_kernel(cfg, msg_hbm, out_hbm, msg_scr, spec_ref, left_scr, vis_scr, in_sem, out_sem):
    n_q, msg_rows, total_frames, rows_dev = cfg
    depth, inputs = spec_ref.shape
    load = pltpu.make_async_copy(msg_hbm, msg_scr, in_sem)
    load.start()
    load.wait()

    for tile in range(inputs // LANES):
        spec_ref[:, tile * LANES : (tile + 1) * LANES] = msg_scr[tile * depth : (tile + 1) * depth]
    spectra = spec_ref[...]
    h, m, l = split_bf16(spectra, 3)
    spare = [jnp.zeros_like(h)] * (-6 % (LANES // depth) if LANES % depth == 0 else 0)
    right = jnp.concatenate([h, m, h, l, h, m] + spare, axis=0)
    anchor = pl.multiple_of(lax.axis_index("frq") * rows_dev, LANES)
    left = spec_ref[:, pl.ds(anchor, rows_dev)] * (1.0 / total_frames)
    row_at = lax.broadcasted_iota(jnp.int32, (msg_rows, rows_dev), 0)
    swapped = jnp.concatenate(
        [
            jnp.where(
                row_at % n_q < n_q // 2,
                pltpu.roll(left[at : at + msg_rows], msg_rows - n_q // 2, 0),
                -pltpu.roll(left[at : at + msg_rows], n_q // 2, 0),
            )
            for at in range(0, depth, msg_rows)
        ],
        axis=0,
    )
    h, m, l = split_bf16(jnp.concatenate([left, swapped], axis=1), 3)
    left_scr[...] = jnp.concatenate([h, h, m, h, l, m] + spare, axis=0).T
    width = 2 * LANES
    copies = []
    for block in range(inputs // width):
        vis = jnp.dot(
            left_scr[...],
            right[:, block * width : (block + 1) * width],
            preferred_element_type=jnp.float32,
        )
        for tile in range(2):
            for part in range(2):
                at = 2 * (2 * block + tile) + part
                vis_scr[at] = vis[
                    part * rows_dev : (part + 1) * rows_dev, tile * LANES : (tile + 1) * LANES
                ]
                copy = pltpu.make_async_copy(vis_scr.at[at], out_hbm.at[:, at], out_sem.at[at])
                copy.start()
                copies.append(copy)
    for copy in copies:
        copy.wait()


def body(n_inp, n_frq, voltages, history, window):
    n_loc, frames, samples = voltages.shape
    taps = window.shape[0]
    inputs = n_loc * n_inp
    channels = CH_DEV * n_inp
    h = history.transpose(1, 0, 2).reshape((taps - 1) * n_loc, samples)
    table = jnp.asarray(dft_rows(channels, samples))

    per_lane = LANES // n_loc
    n_q = 2 * frames // per_lane
    msg_rows = -(-2 * n_q // SUBL) * SUBL
    depth = (n_frq // 2) * per_lane * msg_rows
    x_rows = n_loc * (frames + taps - 1)
    n_groups = n_inp // per_lane
    members = per_lane * n_frq
    half = taps * 2 * channels
    spectra = pl.pallas_call(
        functools.partial(
            spectra_kernel, (n_inp, n_frq, n_loc, frames, taps, channels)
        ),
        out_shape=jax.ShapeDtypeStruct((n_groups * depth, LANES), jnp.float32),
        in_specs=[pl.BlockSpec(memory_space=pl.ANY)] * 4,
        out_specs=pl.BlockSpec(memory_space=pl.ANY),
        scratch_shapes=[
            pltpu.VMEM((n_loc, frames, samples), jnp.bfloat16),
            pltpu.VMEM(((taps - 1) * n_loc, samples), jnp.bfloat16),
            pltpu.VMEM((2 * channels, samples), jnp.float32),
            pltpu.VMEM((taps, samples), jnp.float32),
            pltpu.VMEM((2 * half, samples), jnp.bfloat16),
            pltpu.VMEM((half // LANES, x_rows, LANES), jnp.float32),
            pltpu.VMEM((channels * msg_rows, LANES), jnp.float32),
            pltpu.VMEM((channels * msg_rows, LANES), jnp.float32),
            pltpu.VMEM((channels // members * depth, LANES), jnp.float32),
            pltpu.SemaphoreType.DMA((5,)),
            pltpu.SemaphoreType.DMA,
            pltpu.SemaphoreType.DMA,
            pltpu.SemaphoreType.DMA,
            pltpu.SemaphoreType.DMA,
        ],
        compiler_params=pltpu.CompilerParams(
            collective_id=0, has_side_effects=True, vmem_limit_bytes=60 * 2**20
        ),
        name="spectra_exchange",
    )(voltages, h, table, window)

    rows_dev = inputs // n_frq
    stack = 6 * depth if LANES % depth else -(-6 * depth // LANES) * LANES
    per_row = 2 * inputs // LANES
    vis = pl.pallas_call(
        functools.partial(
            gram_kernel,
            (n_q, msg_rows, frames * n_frq, rows_dev),
        ),
        out_shape=jax.ShapeDtypeStruct((rows_dev, per_row, LANES), jnp.float32),
        in_specs=[pl.BlockSpec(memory_space=pl.ANY)],
        out_specs=pl.BlockSpec(memory_space=pl.ANY),
        scratch_shapes=[
            pltpu.VMEM((n_groups * depth, LANES), jnp.float32),
            pltpu.VMEM((depth, inputs), jnp.float32),
            pltpu.VMEM((2 * rows_dev, stack), jnp.bfloat16),
            pltpu.VMEM((per_row, rows_dev, LANES), jnp.float32),
            pltpu.SemaphoreType.DMA,
            pltpu.SemaphoreType.DMA((per_row,)),
        ],
        compiler_params=pltpu.CompilerParams(vmem_limit_bytes=60 * 2**20),
        name="gram",
    )(spectra)
    return (
        vis.reshape(rows_dev, inputs // LANES, 2, LANES)
        .transpose(0, 2, 1, 3)
        .reshape(rows_dev, 1, 2, inputs)
    )


def solution(mesh):
    return jax.shard_map(
        functools.partial(body, mesh.shape["inp"], mesh.shape["frq"]),
        mesh=mesh,
        in_specs=(P("inp", "frq", None), P("inp", None, None), P()),
        out_specs=P("frq", "inp", None, None),
        check_vma=False,
    )
```

```python
import functools
import math

import jax
import jax.numpy as jnp
import numpy as np
from jax import lax
from jax.experimental import pallas as pl
from jax.experimental.pallas import tpu as pltpu
from jax.sharding import PartitionSpec as P

CH_DEV = 1
LANES = 128
SUBL = 8
MESH = pl.DeviceIdType.MESH


def dft_rows(channels, samples):
    first_bin = (samples // 2 - channels) // 2
    bins = np.arange(channels, dtype=np.int64) + first_bin
    turns = bins[:, None] * np.arange(samples, dtype=np.int64)[None, :] % samples
    phases = turns * (2.0 * math.pi / samples)
    table = np.concatenate([np.cos(phases), -np.sin(phases)], axis=0) / math.sqrt(samples)
    return table.astype(np.float32)


def split_bf16(value, pieces):
    out = []
    for _ in range(pieces):
        piece = value.astype(jnp.bfloat16)
        out.append(piece)
        value = value - piece.astype(jnp.float32)
    return out


def to_others(n_inp, n_frq, my_inp, my_frq, act):
    def group(ahead, low):
        to_inp = lax.rem(my_inp + ahead, n_inp)
        for turn in range(low, n_frq):
            act(to_inp, lax.rem(my_frq + turn, n_frq))

    if n_inp * n_frq <= 32:
        for step in range(n_inp - 1):
            group((n_inp // 2 + step) % n_inp if step < n_inp // 2 else n_inp - 1 - step, 0)
    else:
        lax.fori_loop(1, n_inp, lambda step, carry: (group(step, 0), carry)[1], 0)
    group(0, 1)


def spectra_kernel(
    cfg, x_hbm, h_hbm, table_hbm, window_hbm, out_hbm,
    x_scr, h_scr, table_scr, window_scr, mat_scr, z_scr, msg_scr,
    in_sem, send_sem, recv_sem,
):
    n_inp, n_frq, n_loc, frames, taps, channels = cfg
    n_dev = n_inp * n_frq
    my_inp = lax.axis_index("inp")
    my_frq = lax.axis_index("frq")
    me = my_inp * n_frq + my_frq
    v_rows = n_loc * frames
    loads = [
        pltpu.make_async_copy(table_hbm, table_scr, in_sem.at[0]),
        pltpu.make_async_copy(window_hbm, window_scr, in_sem.at[1]),
        pltpu.make_async_copy(h_hbm, h_scr, in_sem.at[2]),
    ] + [
        pltpu.make_async_copy(x_hbm.at[:, tile], x_scr.at[tile], in_sem.at[4 + tile])
        for tile in range(x_hbm.shape[1])
    ]
    for load in loads:
        load.start()

    barrier = pltpu.get_barrier_semaphore()

    def greet(to_inp, to_frq):
        pl.semaphore_signal(barrier, inc=1, device_id=(to_inp, to_frq), device_id_type=MESH)

    to_others(n_inp, n_frq, my_inp, my_frq, greet)

    loads[0].wait()
    loads[1].wait()
    group = 2 * channels
    for tap in range(taps):
        hi, lo = split_bf16(window_scr[tap : tap + 1, :] * table_scr[...], 2)
        mat_scr[tap * group : (tap + 1) * group, :] = hi
        mat_scr[(taps + tap) * group : (taps + tap + 1) * group, :] = lo
    half = taps * group
    tiles = half // LANES

    loads[2].wait()
    for load in loads[3:]:
        load.wait()
    flat = x_scr.reshape(x_scr.shape[0], v_rows, LANES)
    rows = jnp.concatenate([flat[tile] for tile in range(x_scr.shape[0])], axis=1)
    rows = jnp.concatenate([rows, h_scr[...]], axis=0)
    z = lax.dot_general(
        rows, mat_scr[...], (((1,), (1,)), ((), ())), preferred_element_type=jnp.float32
    )
    for tile in range(tiles):
        z_scr[tile] = (
            z[:, tile * LANES : (tile + 1) * LANES]
            + z[:, half + tile * LANES : half + (tile + 1) * LANES]
        )

    first = my_frq == 0

    def frame(tile, u):
        if u >= frames:
            return None
        if u >= 0:
            return z_scr[tile, pl.ds(u, n_loc, stride=frames), :]
        at = v_rows + (u + taps - 1) * n_loc
        rows = z_scr[tile, at : at + n_loc, :]
        return jnp.where(first, rows, 0.0)

    held = {(tile, u): frame(tile, u) for tile in range(tiles) for u in range(1 - taps, frames)}
    per_tile = LANES // group
    lane_group = lax.broadcasted_iota(jnp.int32, (n_loc, LANES), 1) // group
    per_lane = LANES // n_loc
    n_q = 2 * frames // per_lane
    half_q = n_q // 2
    msg_rows = msg_scr.shape[0] // channels

    def frame_products(tile, t):
        total = jnp.zeros((n_loc, LANES), jnp.float32)
        for g in range(per_tile):
            u = t - (taps - 1) + tile * per_tile + g
            part = held.get((tile, u))
            if part is not None:
                total = jnp.where(lane_group == g, part, total)
        return total

    for q in range(n_q):
        acc = None
        for tile in range(tiles):
            block = jnp.concatenate(
                [frame_products(tile, q * per_lane + c) for c in range(per_lane)], axis=0
            ).T
            for g in range(per_tile):
                part = block[g * group : (g + 1) * group]
                acc = part if acc is None else acc + part
        for part in range(2):
            for jb in range(channels // SUBL):
                row = part * channels + jb * SUBL
                at = q // half_q * n_q + part * half_q + q % half_q
                msg_scr[pl.ds(jb * SUBL * msg_rows + at, SUBL, stride=msg_rows), :] = acc[
                    row : row + SUBL
                ]
    if msg_rows > 2 * n_q:
        for row in range(2 * n_q, msg_rows):
            for jb in range(channels // SUBL):
                msg_scr[pl.ds(jb * SUBL * msg_rows + row, SUBL, stride=msg_rows), :] = jnp.zeros(
                    (SUBL, LANES), jnp.float32
                )

    own_rows = n_q if n_q % 4 == 0 else msg_rows

    def exchange(rows, waited):
        my_slot = out_hbm.at[pl.ds(pl.multiple_of(me * msg_rows, SUBL), rows)]

        def message(to_inp):
            return msg_scr.at[pl.ds(pl.multiple_of(to_inp * msg_rows, SUBL), rows)]

        def send(to_inp, to_frq):
            pltpu.make_async_remote_copy(
                src_ref=message(to_inp),
                dst_ref=my_slot,
                send_sem=send_sem,
                recv_sem=recv_sem,
                device_id=(to_inp, to_frq),
                device_id_type=MESH,
            ).start()

        def bytes_of(count):
            return pltpu.make_async_remote_copy(
                src_ref=out_hbm.at[pl.ds(0, count)],
                dst_ref=out_hbm.at[pl.ds(0, count)],
                send_sem=send_sem,
                recv_sem=recv_sem,
                device_id=(my_inp, my_frq),
                device_id_type=MESH,
            )

        mine = pltpu.make_async_copy(message(my_inp), my_slot, in_sem.at[3])
        mine.start()
        to_others(n_inp, n_frq, my_inp, my_frq, send)
        bytes_of(waited).wait_recv()
        bytes_of((n_dev - 1) * rows).wait_send()
        mine.wait()

    pl.semaphore_wait(barrier, n_dev - 1)
    arriving = n_inp * ((n_frq - 1) * msg_rows + own_rows)
    last = my_frq == n_frq - 1
    pl.when(last)(lambda: exchange(own_rows, arriving - own_rows))
    pl.when(jnp.logical_not(last))(lambda: exchange(msg_rows, arriving - msg_rows))


def row_blocks(rows):
    small = SUBL * SUBL
    edges = [0, small] + list(range(2 * small, rows + 1, 2 * small))
    return [(low, high - low) for low, high in zip(edges, edges[1:])]


def gram_kernel(
    cfg, msg_hbm, out_hbm, msg_scr, spec_ref, left_scr, right_scr, vis_scr,
    in_sem, out_sem,
):
    n_inp, n_frq, n_loc, n_q, msg_rows, total_frames, rows_dev = cfg
    depth, inputs = spec_ref.shape
    per_lane = LANES // n_loc
    load = pltpu.make_async_copy(msg_hbm, msg_scr, in_sem)
    load.start()
    load.wait()

    row = lax.broadcasted_iota(jnp.int32, (msg_rows, LANES), 0)
    own = row < n_q
    later = (row >= n_q) & (row < 2 * n_q)
    lane_part = lax.broadcasted_iota(jnp.int32, (msg_rows, LANES), 1) // n_loc

    for m in range(n_inp // per_lane):
        msgs = [
            [
                msg_scr[((m * per_lane + e) * n_frq + f) * msg_rows :
                         ((m * per_lane + e) * n_frq + f + 1) * msg_rows, :]
                for e in range(per_lane)
            ]
            for f in range(n_frq)
        ]
        for c in range(per_lane):
            lined = []
            for f in range(n_frq):
                tile = None
                for e in range(per_lane):
                    turn = (e - c) * n_loc % LANES
                    piece = pltpu.roll(msgs[f][e], turn, 1) if turn else msgs[f][e]
                    tile = piece if tile is None else jnp.where(lane_part == e, piece, tile)
                lined.append(tile)
            for pair in range(n_frq // 2):
                even, odd = lined[2 * pair], lined[2 * pair + 1]
                total = even + jnp.where(later, pltpu.roll(odd, n_q, 0), 0.0)
                if pair:
                    before = pltpu.roll(lined[2 * pair - 1], msg_rows - n_q, 0)
                    total = total + jnp.where(own, before, 0.0)
                at = (pair * per_lane + c) * msg_rows
                spec_ref[at : at + msg_rows, m * LANES : (m + 1) * LANES] = total

    spectra = spec_ref[...]
    h, m, l = split_bf16(spectra, 3)
    spare = [jnp.zeros_like(h)] * (-6 % (LANES // depth) if LANES % depth == 0 else 0)
    right = jnp.concatenate([h, m, h, l, h, m] + spare, axis=0)
    anchor = pl.multiple_of(lax.axis_index("frq") * rows_dev, LANES)
    left = spec_ref[:, pl.ds(anchor, rows_dev)] * (1.0 / total_frames)
    row_at = lax.broadcasted_iota(jnp.int32, (msg_rows, rows_dev), 0)
    swapped = jnp.concatenate(
        [
            jnp.where(
                row_at % n_q < n_q // 2,
                pltpu.roll(left[at : at + msg_rows], msg_rows - n_q // 2, 0),
                -pltpu.roll(left[at : at + msg_rows], n_q // 2, 0),
            )
            for at in range(0, depth, msg_rows)
        ],
        axis=0,
    )
    h, m, l = split_bf16(jnp.concatenate([left, swapped], axis=1), 3)
    left_scr[...] = jnp.concatenate([h, h, m, h, l, m] + spare, axis=0).T
    right_scr[...] = right
    per_row = 2 * inputs // LANES
    copies = []
    for row, block in row_blocks(rows_dev):
        sides = [
            left_scr[part * rows_dev + row : part * rows_dev + row + block, :]
            for part in range(2)
        ]
        vis = jnp.dot(
            jnp.concatenate(sides, axis=0), right_scr[...], preferred_element_type=jnp.float32
        )
        for part in range(2):
            for r in range(0, block, SUBL):
                for tile in range(inputs // LANES):
                    at = (row + r) * per_row + 2 * tile + part
                    vis_scr[pl.ds(at, SUBL, stride=per_row), :] = vis[
                        part * block + r : part * block + r + SUBL,
                        tile * LANES : (tile + 1) * LANES,
                    ]
        rows = pl.ds(row * per_row, block * per_row)
        copies.append(
            pltpu.make_async_copy(vis_scr.at[rows], out_hbm.at[rows], out_sem.at[len(copies)])
        )
        copies[-1].start()
    for copy in copies:
        copy.wait()


def body(n_inp, n_frq, voltages, history, window):
    n_loc, frames, samples = voltages.shape
    taps = window.shape[0]
    inputs = n_loc * n_inp
    channels = CH_DEV * n_inp
    x = voltages.reshape(n_loc, frames, samples // LANES, LANES).transpose(0, 2, 1, 3)
    h = history.transpose(1, 0, 2).reshape((taps - 1) * n_loc, samples)
    table = jnp.asarray(dft_rows(channels, samples))

    per_lane = LANES // n_loc
    n_q = 2 * frames // per_lane
    msg_rows = -(-2 * n_q // SUBL) * SUBL
    depth = (n_frq // 2) * per_lane * msg_rows
    x_rows = n_loc * (frames + taps - 1)
    n_dev = n_inp * n_frq
    half = taps * 2 * channels
    spectra = pl.pallas_call(
        functools.partial(
            spectra_kernel, (n_inp, n_frq, n_loc, frames, taps, channels)
        ),
        out_shape=jax.ShapeDtypeStruct((n_dev * msg_rows, LANES), jnp.float32),
        in_specs=[pl.BlockSpec(memory_space=pl.ANY)] * 4,
        out_specs=pl.BlockSpec(memory_space=pl.ANY),
        scratch_shapes=[
            pltpu.VMEM((samples // LANES, n_loc, frames, LANES), jnp.bfloat16),
            pltpu.VMEM(((taps - 1) * n_loc, samples), jnp.bfloat16),
            pltpu.VMEM((2 * channels, samples), jnp.float32),
            pltpu.VMEM((taps, samples), jnp.float32),
            pltpu.VMEM((2 * half, samples), jnp.bfloat16),
            pltpu.VMEM((half // LANES, x_rows, LANES), jnp.float32),
            pltpu.VMEM((channels * msg_rows, LANES), jnp.float32),
            pltpu.SemaphoreType.DMA((4 + samples // LANES,)),
            pltpu.SemaphoreType.DMA,
            pltpu.SemaphoreType.DMA,
        ],
        compiler_params=pltpu.CompilerParams(
            collective_id=0, has_side_effects=True, vmem_limit_bytes=60 * 2**20
        ),
        name="spectra_exchange",
    )(x, h, table, window)

    rows_dev = inputs // n_frq
    stack = 6 * depth if LANES % depth else -(-6 * depth // LANES) * LANES
    per_row = 2 * inputs // LANES
    vis = pl.pallas_call(
        functools.partial(
            gram_kernel,
            (n_inp, n_frq, n_loc, n_q, msg_rows, frames * n_frq, rows_dev),
        ),
        out_shape=jax.ShapeDtypeStruct((rows_dev * per_row, LANES), jnp.float32),
        in_specs=[pl.BlockSpec(memory_space=pl.ANY)],
        out_specs=pl.BlockSpec(memory_space=pl.ANY),
        scratch_shapes=[
            pltpu.VMEM((n_dev * msg_rows, LANES), jnp.float32),
            pltpu.VMEM((depth, inputs), jnp.float32),
            pltpu.VMEM((2 * rows_dev, stack), jnp.bfloat16),
            pltpu.VMEM((stack, inputs), jnp.bfloat16),
            pltpu.VMEM((rows_dev * per_row, LANES), jnp.float32),
            pltpu.SemaphoreType.DMA,
            pltpu.SemaphoreType.DMA((len(row_blocks(rows_dev)),)),
        ],
        compiler_params=pltpu.CompilerParams(vmem_limit_bytes=60 * 2**20),
        name="gram",
    )(spectra)
    return (
        vis.reshape(rows_dev, inputs // LANES, 2, LANES)
        .transpose(0, 2, 1, 3)
        .reshape(rows_dev, 1, 2, inputs)
    )


def solution(mesh):
    return jax.shard_map(
        functools.partial(body, mesh.shape["inp"], mesh.shape["frq"]),
        mesh=mesh,
        in_specs=(P("inp", "frq", None), P("inp", None, None), P()),
        out_specs=P("frq", "inp", None, None),
        check_vma=False,
    )
```

```python
import functools
import math

import jax
import jax.numpy as jnp
import numpy as np
from jax import lax
from jax.experimental import pallas as pl
from jax.experimental.pallas import tpu as pltpu
from jax.sharding import PartitionSpec as P

CH_DEV = 1
LANES = 128
SUBL = 8
MESH = pl.DeviceIdType.MESH


def dft_rows(channels, samples):
    first_bin = (samples // 2 - channels) // 2
    bins = np.arange(channels, dtype=np.int64) + first_bin
    turns = bins[:, None] * np.arange(samples, dtype=np.int64)[None, :] % samples
    phases = turns * (2.0 * math.pi / samples)
    table = np.concatenate([np.cos(phases), -np.sin(phases)], axis=0) / math.sqrt(samples)
    return table.astype(np.float32)


def split_bf16(value, pieces):
    out = []
    for _ in range(pieces):
        piece = value.astype(jnp.bfloat16)
        out.append(piece)
        value = value - piece.astype(jnp.float32)
    return out


def others(n_inp, n_frq, my_inp, my_frq):
    found = []
    for step in range(n_inp):
        ahead = (n_inp // 2 + step) % n_inp if step < n_inp // 2 else n_inp - 1 - step
        to_inp = lax.rem(my_inp + ahead, n_inp)
        for turn in range(0 if ahead else 1, n_frq):
            found.append((to_inp, lax.rem(my_frq + turn, n_frq)))
    return found


def spectra_kernel(
    cfg, x_hbm, h_hbm, table_hbm, window_hbm, out_hbm,
    x_scr, h_scr, table_scr, window_scr, mat_scr, z_scr, msg_scr,
    in_sem, send_sem, recv_sem,
):
    n_inp, n_frq, n_loc, frames, taps, channels = cfg
    n_dev = n_inp * n_frq
    my_inp = lax.axis_index("inp")
    my_frq = lax.axis_index("frq")
    me = my_inp * n_frq + my_frq
    v_rows = n_loc * frames
    loads = [
        pltpu.make_async_copy(table_hbm, table_scr, in_sem.at[0]),
        pltpu.make_async_copy(window_hbm, window_scr, in_sem.at[1]),
        pltpu.make_async_copy(h_hbm, h_scr, in_sem.at[2]),
    ] + [
        pltpu.make_async_copy(x_hbm.at[:, tile], x_scr.at[tile], in_sem.at[4 + tile])
        for tile in range(x_hbm.shape[1])
    ]
    for load in loads:
        load.start()

    barrier = pltpu.get_barrier_semaphore()

    devices = others(n_inp, n_frq, my_inp, my_frq)

    def greet(some):
        for device in some:
            pl.semaphore_signal(barrier, inc=1, device_id=device, device_id_type=MESH)

    greet(devices[: n_dev // 2])

    loads[0].wait()
    loads[1].wait()
    group = 2 * channels
    for tap in range(taps):
        hi, lo = split_bf16(window_scr[tap : tap + 1, :] * table_scr[...], 2)
        mat_scr[tap * group : (tap + 1) * group, :] = hi
        mat_scr[(taps + tap) * group : (taps + tap + 1) * group, :] = lo
        greet(devices[n_dev // 2 :][tap::taps])
    half = taps * group
    tiles = half // LANES

    loads[2].wait()
    for load in loads[3:]:
        load.wait()
    flat = x_scr.reshape(x_scr.shape[0], v_rows, LANES)
    rows = jnp.concatenate([flat[tile] for tile in range(x_scr.shape[0])], axis=1)
    rows = jnp.concatenate([rows, h_scr[...]], axis=0)
    z = lax.dot_general(
        rows, mat_scr[...], (((1,), (1,)), ((), ())), preferred_element_type=jnp.float32
    )
    for tile in range(tiles):
        z_scr[tile] = (
            z[:, tile * LANES : (tile + 1) * LANES]
            + z[:, half + tile * LANES : half + (tile + 1) * LANES]
        )

    first = my_frq == 0

    def frame(tile, u):
        if u >= frames:
            return None
        if u >= 0:
            return z_scr[tile, pl.ds(u, n_loc, stride=frames), :]
        at = v_rows + (u + taps - 1) * n_loc
        rows = z_scr[tile, at : at + n_loc, :]
        return jnp.where(first, rows, 0.0)

    held = {(tile, u): frame(tile, u) for tile in range(tiles) for u in range(1 - taps, frames)}
    per_tile = LANES // group
    lane_group = lax.broadcasted_iota(jnp.int32, (n_loc, LANES), 1) // group
    per_lane = LANES // n_loc
    n_q = 2 * frames // per_lane
    half_q = n_q // 2
    msg_rows = msg_scr.shape[0] // channels

    def frame_products(tile, t):
        total = jnp.zeros((n_loc, LANES), jnp.float32)
        for g in range(per_tile):
            u = t - (taps - 1) + tile * per_tile + g
            part = held.get((tile, u))
            if part is not None:
                total = jnp.where(lane_group == g, part, total)
        return total

    for q in range(n_q):
        acc = None
        for tile in range(tiles):
            block = jnp.concatenate(
                [frame_products(tile, q * per_lane + c) for c in range(per_lane)], axis=0
            ).T
            for g in range(per_tile):
                part = block[g * group : (g + 1) * group]
                acc = part if acc is None else acc + part
        for part in range(2):
            for jb in range(channels // SUBL):
                row = part * channels + jb * SUBL
                at = q // half_q * n_q + part * half_q + q % half_q
                msg_scr[pl.ds(jb * SUBL * msg_rows + at, SUBL, stride=msg_rows), :] = acc[
                    row : row + SUBL
                ]
    if msg_rows > 2 * n_q:
        for row in range(2 * n_q, msg_rows):
            for jb in range(channels // SUBL):
                msg_scr[pl.ds(jb * SUBL * msg_rows + row, SUBL, stride=msg_rows), :] = jnp.zeros(
                    (SUBL, LANES), jnp.float32
                )

    pl.semaphore_wait(barrier, n_dev - 1)
    my_slot = out_hbm.at[pl.ds(pl.multiple_of(me * msg_rows, SUBL), msg_rows)]

    def message(to_inp):
        return msg_scr.at[pl.ds(pl.multiple_of(to_inp * msg_rows, SUBL), msg_rows)]

    for device in devices:
        pltpu.make_async_remote_copy(
            src_ref=message(device[0]),
            dst_ref=my_slot,
            send_sem=send_sem,
            recv_sem=recv_sem,
            device_id=device,
            device_id_type=MESH,
        ).start()
    mine = pltpu.make_async_copy(message(my_inp), my_slot, in_sem.at[3])
    mine.start()
    rest = out_hbm.at[pl.ds(0, (n_dev - 1) * msg_rows)]
    everything = pltpu.make_async_remote_copy(
        src_ref=rest,
        dst_ref=rest,
        send_sem=send_sem,
        recv_sem=recv_sem,
        device_id=(my_inp, my_frq),
        device_id_type=MESH,
    )
    mine.wait()
    everything.wait_recv()
    everything.wait_send()


def row_blocks(rows):
    edges = [0, LANES // 4, LANES // 2] + list(range(LANES, rows + 1, LANES))
    return [(low, high - low) for low, high in zip(edges, edges[1:])]


def gram_kernel(
    cfg, msg_hbm, out_hbm, msg_scr, spec_ref, left_scr, right_scr, vis_scr,
    in_sem, out_sem,
):
    n_inp, n_frq, n_loc, n_q, msg_rows, total_frames, rows_dev = cfg
    depth, inputs = spec_ref.shape
    per_lane = LANES // n_loc
    load = pltpu.make_async_copy(msg_hbm, msg_scr, in_sem)
    load.start()
    load.wait()

    row = lax.broadcasted_iota(jnp.int32, (msg_rows, LANES), 0)
    own = row < n_q
    later = (row >= n_q) & (row < 2 * n_q)
    lane_part = lax.broadcasted_iota(jnp.int32, (msg_rows, LANES), 1) // n_loc

    for m in range(n_inp // per_lane):
        msgs = [
            [
                msg_scr[((m * per_lane + e) * n_frq + f) * msg_rows :
                         ((m * per_lane + e) * n_frq + f + 1) * msg_rows, :]
                for e in range(per_lane)
            ]
            for f in range(n_frq)
        ]
        for c in range(per_lane):
            lined = []
            for f in range(n_frq):
                tile = None
                for e in range(per_lane):
                    turn = (e - c) * n_loc % LANES
                    piece = pltpu.roll(msgs[f][e], turn, 1) if turn else msgs[f][e]
                    tile = piece if tile is None else jnp.where(lane_part == e, piece, tile)
                lined.append(tile)
            for pair in range(n_frq // 2):
                even, odd = lined[2 * pair], lined[2 * pair + 1]
                total = even + jnp.where(later, pltpu.roll(odd, n_q, 0), 0.0)
                if pair:
                    before = pltpu.roll(lined[2 * pair - 1], msg_rows - n_q, 0)
                    total = total + jnp.where(own, before, 0.0)
                at = (pair * per_lane + c) * msg_rows
                spec_ref[at : at + msg_rows, m * LANES : (m + 1) * LANES] = total

    spectra = spec_ref[...]
    h, m, l = split_bf16(spectra, 3)
    spare = [jnp.zeros_like(h)] * (-6 % (LANES // depth) if LANES % depth == 0 else 0)
    right = jnp.concatenate([h, m, h, l, h, m] + spare, axis=0)
    anchor = pl.multiple_of(lax.axis_index("frq") * rows_dev, LANES)
    left = spec_ref[:, pl.ds(anchor, rows_dev)] * (1.0 / total_frames)
    row_at = lax.broadcasted_iota(jnp.int32, (msg_rows, rows_dev), 0)
    swapped = jnp.concatenate(
        [
            jnp.where(
                row_at % n_q < n_q // 2,
                pltpu.roll(left[at : at + msg_rows], msg_rows - n_q // 2, 0),
                -pltpu.roll(left[at : at + msg_rows], n_q // 2, 0),
            )
            for at in range(0, depth, msg_rows)
        ],
        axis=0,
    )
    h, m, l = split_bf16(jnp.concatenate([left, swapped], axis=1), 3)
    left_scr[...] = jnp.concatenate([h, h, m, h, l, m] + spare, axis=0).T
    right_scr[...] = right
    per_row = 2 * inputs // LANES
    copies = []
    for row, block in row_blocks(rows_dev):
        sides = [
            left_scr[part * rows_dev + row : part * rows_dev + row + block, :]
            for part in range(2)
        ]
        vis = jnp.dot(
            jnp.concatenate(sides, axis=0), right_scr[...], preferred_element_type=jnp.float32
        )
        for part in range(2):
            for r in range(0, block, SUBL):
                for tile in range(inputs // LANES):
                    at = (row + r) * per_row + 2 * tile + part
                    vis_scr[pl.ds(at, SUBL, stride=per_row), :] = vis[
                        part * block + r : part * block + r + SUBL,
                        tile * LANES : (tile + 1) * LANES,
                    ]
        rows = pl.ds(row * per_row, block * per_row)
        copies.append(
            pltpu.make_async_copy(vis_scr.at[rows], out_hbm.at[rows], out_sem.at[len(copies)])
        )
        copies[-1].start()
    for copy in copies:
        copy.wait()


def body(n_inp, n_frq, voltages, history, window):
    n_loc, frames, samples = voltages.shape
    taps = window.shape[0]
    inputs = n_loc * n_inp
    channels = CH_DEV * n_inp
    x = voltages.reshape(n_loc, frames, samples // LANES, LANES).transpose(0, 2, 1, 3)
    h = history.transpose(1, 0, 2).reshape((taps - 1) * n_loc, samples)
    table = jnp.asarray(dft_rows(channels, samples))

    per_lane = LANES // n_loc
    n_q = 2 * frames // per_lane
    msg_rows = -(-2 * n_q // SUBL) * SUBL
    depth = (n_frq // 2) * per_lane * msg_rows
    x_rows = n_loc * (frames + taps - 1)
    n_dev = n_inp * n_frq
    half = taps * 2 * channels
    spectra = pl.pallas_call(
        functools.partial(
            spectra_kernel, (n_inp, n_frq, n_loc, frames, taps, channels)
        ),
        out_shape=jax.ShapeDtypeStruct((n_dev * msg_rows, LANES), jnp.float32),
        in_specs=[pl.BlockSpec(memory_space=pl.ANY)] * 4,
        out_specs=pl.BlockSpec(memory_space=pl.ANY),
        scratch_shapes=[
            pltpu.VMEM((samples // LANES, n_loc, frames, LANES), jnp.bfloat16),
            pltpu.VMEM(((taps - 1) * n_loc, samples), jnp.bfloat16),
            pltpu.VMEM((2 * channels, samples), jnp.float32),
            pltpu.VMEM((taps, samples), jnp.float32),
            pltpu.VMEM((2 * half, samples), jnp.bfloat16),
            pltpu.VMEM((half // LANES, x_rows, LANES), jnp.float32),
            pltpu.VMEM((channels * msg_rows, LANES), jnp.float32),
            pltpu.SemaphoreType.DMA((4 + samples // LANES,)),
            pltpu.SemaphoreType.DMA,
            pltpu.SemaphoreType.DMA,
        ],
        compiler_params=pltpu.CompilerParams(
            collective_id=0, has_side_effects=True, vmem_limit_bytes=60 * 2**20
        ),
        name="spectra_exchange",
    )(x, h, table, window)

    rows_dev = inputs // n_frq
    stack = 6 * depth if LANES % depth else -(-6 * depth // LANES) * LANES
    per_row = 2 * inputs // LANES
    vis = pl.pallas_call(
        functools.partial(
            gram_kernel,
            (n_inp, n_frq, n_loc, n_q, msg_rows, frames * n_frq, rows_dev),
        ),
        out_shape=jax.ShapeDtypeStruct((rows_dev * per_row, LANES), jnp.float32),
        in_specs=[pl.BlockSpec(memory_space=pl.ANY)],
        out_specs=pl.BlockSpec(memory_space=pl.ANY),
        scratch_shapes=[
            pltpu.VMEM((n_dev * msg_rows, LANES), jnp.float32),
            pltpu.VMEM((depth, inputs), jnp.float32),
            pltpu.VMEM((2 * rows_dev, stack), jnp.bfloat16),
            pltpu.VMEM((stack, inputs), jnp.bfloat16),
            pltpu.VMEM((rows_dev * per_row, LANES), jnp.float32),
            pltpu.SemaphoreType.DMA,
            pltpu.SemaphoreType.DMA((len(row_blocks(rows_dev)),)),
        ],
        compiler_params=pltpu.CompilerParams(vmem_limit_bytes=60 * 2**20),
        name="gram",
    )(spectra)
    return (
        vis.reshape(rows_dev, inputs // LANES, 2, LANES)
        .transpose(0, 2, 1, 3)
        .reshape(rows_dev, 1, 2, inputs)
    )


def solution(mesh):
    return jax.shard_map(
        functools.partial(body, mesh.shape["inp"], mesh.shape["frq"]),
        mesh=mesh,
        in_specs=(P("inp", "frq", None), P("inp", None, None), P()),
        out_specs=P("frq", "inp", None, None),
        check_vma=False,
    )
```

```python
import functools
import math

import jax
import jax.numpy as jnp
import numpy as np
from jax import lax
from jax.experimental import pallas as pl
from jax.experimental.pallas import tpu as pltpu
from jax.sharding import PartitionSpec as P

CH_DEV = 1
LANES = 128
SUBL = 8
MESH = pl.DeviceIdType.MESH


def dft_rows(channels, samples):
    first_bin = (samples // 2 - channels) // 2
    bins = np.arange(channels, dtype=np.int64) + first_bin
    turns = bins[:, None] * np.arange(samples, dtype=np.int64)[None, :] % samples
    phases = turns * (2.0 * math.pi / samples)
    table = np.concatenate([np.cos(phases), -np.sin(phases)], axis=0) / math.sqrt(samples)
    return table.astype(np.float32)


def split_bf16(value, pieces):
    out = []
    for _ in range(pieces):
        piece = value.astype(jnp.bfloat16)
        out.append(piece)
        value = value - piece.astype(jnp.float32)
    return out


def ahead_of(index, steps, size):
    moved = index + steps
    return jnp.where(moved >= size, moved - size, moved)


def to_others(n_inp, n_frq, my_inp, my_frq, act):
    def group(ahead, low):
        to_inp = ahead_of(my_inp, ahead, n_inp)
        for turn in range(low, n_frq):
            act(to_inp, ahead_of(my_frq, turn, n_frq) if turn else my_frq)

    if n_inp * n_frq <= 32:
        for step in range(n_inp - 1):
            group((n_inp // 2 + step) % n_inp if step < n_inp // 2 else n_inp - 1 - step, 0)
    else:
        lax.fori_loop(1, n_inp, lambda step, carry: (group(step, 0), carry)[1], 0)
    for turn in range(1, n_frq):
        act(my_inp, ahead_of(my_frq, turn, n_frq))


def spectra_kernel(
    cfg, x_hbm, h_hbm, table_hbm, window_hbm, out_hbm,
    x_scr, h_scr, table_scr, window_scr, mat_scr, z_scr, msg_scr,
    in_sem, send_sem, recv_sem,
):
    n_inp, n_frq, n_loc, frames, taps, channels = cfg
    n_dev = n_inp * n_frq
    my_inp = lax.axis_index("inp")
    my_frq = lax.axis_index("frq")
    me = my_inp * n_frq + my_frq
    v_rows = n_loc * frames
    loads = [
        pltpu.make_async_copy(table_hbm, table_scr, in_sem.at[0]),
        pltpu.make_async_copy(window_hbm, window_scr, in_sem.at[1]),
        pltpu.make_async_copy(h_hbm, h_scr, in_sem.at[2]),
    ] + [
        pltpu.make_async_copy(x_hbm.at[:, tile], x_scr.at[tile], in_sem.at[4 + tile])
        for tile in range(x_hbm.shape[1])
    ]
    for load in loads:
        load.start()

    barrier = pltpu.get_barrier_semaphore()

    def greet(to_inp, to_frq):
        pl.semaphore_signal(barrier, inc=1, device_id=(to_inp, to_frq), device_id_type=MESH)

    to_others(n_inp, n_frq, my_inp, my_frq, greet)

    loads[0].wait()
    loads[1].wait()
    group = 2 * channels
    for tap in range(taps):
        hi, lo = split_bf16(window_scr[tap : tap + 1, :] * table_scr[...], 2)
        mat_scr[tap * group : (tap + 1) * group, :] = hi
        mat_scr[(taps + tap) * group : (taps + tap + 1) * group, :] = lo
    half = taps * group
    tiles = half // LANES

    loads[2].wait()
    for load in loads[3:]:
        load.wait()
    flat = x_scr.reshape(x_scr.shape[0], v_rows, LANES)
    rows = jnp.concatenate([flat[tile] for tile in range(x_scr.shape[0])], axis=1)
    rows = jnp.concatenate([rows, h_scr[...]], axis=0)
    z = lax.dot_general(
        rows, mat_scr[...], (((1,), (1,)), ((), ())), preferred_element_type=jnp.float32
    )
    for tile in range(tiles):
        z_scr[tile] = (
            z[:, tile * LANES : (tile + 1) * LANES]
            + z[:, half + tile * LANES : half + (tile + 1) * LANES]
        )

    first = my_frq == 0

    def frame(tile, u):
        if u >= frames:
            return None
        if u >= 0:
            return z_scr[tile, pl.ds(u, n_loc, stride=frames), :]
        at = v_rows + (u + taps - 1) * n_loc
        rows = z_scr[tile, at : at + n_loc, :]
        return jnp.where(first, rows, 0.0)

    held = {(tile, u): frame(tile, u) for tile in range(tiles) for u in range(1 - taps, frames)}
    per_tile = LANES // group
    lane_group = lax.broadcasted_iota(jnp.int32, (n_loc, LANES), 1) // group
    per_lane = LANES // n_loc
    n_q = 2 * frames // per_lane
    half_q = n_q // 2
    msg_rows = msg_scr.shape[0] // channels

    def frame_products(tile, t):
        total = jnp.zeros((n_loc, LANES), jnp.float32)
        for g in range(per_tile):
            u = t - (taps - 1) + tile * per_tile + g
            part = held.get((tile, u))
            if part is not None:
                total = jnp.where(lane_group == g, part, total)
        return total

    for q in range(n_q):
        acc = None
        for tile in range(tiles):
            block = jnp.concatenate(
                [frame_products(tile, q * per_lane + c) for c in range(per_lane)], axis=0
            ).T
            for g in range(per_tile):
                part = block[g * group : (g + 1) * group]
                acc = part if acc is None else acc + part
        for part in range(2):
            for jb in range(channels // SUBL):
                row = part * channels + jb * SUBL
                at = q // half_q * n_q + part * half_q + q % half_q
                msg_scr[pl.ds(jb * SUBL * msg_rows + at, SUBL, stride=msg_rows), :] = acc[
                    row : row + SUBL
                ]
    if msg_rows > 2 * n_q:
        for row in range(2 * n_q, msg_rows):
            for jb in range(channels // SUBL):
                msg_scr[pl.ds(jb * SUBL * msg_rows + row, SUBL, stride=msg_rows), :] = jnp.zeros(
                    (SUBL, LANES), jnp.float32
                )

    own_rows = n_q if n_q % 4 == 0 else msg_rows

    def exchange(rows, waited):
        my_slot = out_hbm.at[pl.ds(pl.multiple_of(me * msg_rows, SUBL), rows)]

        def message(to_inp):
            return msg_scr.at[pl.ds(pl.multiple_of(to_inp * msg_rows, SUBL), rows)]

        def send(to_inp, to_frq):
            pltpu.make_async_remote_copy(
                src_ref=message(to_inp),
                dst_ref=my_slot,
                send_sem=send_sem,
                recv_sem=recv_sem,
                device_id=(to_inp, to_frq),
                device_id_type=MESH,
            ).start()

        def bytes_of(count):
            return pltpu.make_async_remote_copy(
                src_ref=out_hbm.at[pl.ds(0, count)],
                dst_ref=out_hbm.at[pl.ds(0, count)],
                send_sem=send_sem,
                recv_sem=recv_sem,
                device_id=(my_inp, my_frq),
                device_id_type=MESH,
            )

        mine = pltpu.make_async_copy(message(my_inp), my_slot, in_sem.at[3])
        mine.start()
        to_others(n_inp, n_frq, my_inp, my_frq, send)
        bytes_of(waited).wait_recv()
        bytes_of((n_dev - 1) * rows).wait_send()
        mine.wait()

    pl.semaphore_wait(barrier, n_dev - 1)
    arriving = n_inp * ((n_frq - 1) * msg_rows + own_rows)
    last = my_frq == n_frq - 1
    pl.when(last)(lambda: exchange(own_rows, arriving - own_rows))
    pl.when(jnp.logical_not(last))(lambda: exchange(msg_rows, arriving - msg_rows))


def row_blocks(rows):
    small = SUBL * SUBL
    edges = [0, small] + list(range(2 * small, rows + 1, 2 * small))
    return [(low, high - low) for low, high in zip(edges, edges[1:])]


def gram_kernel(
    cfg, msg_hbm, out_hbm, msg_scr, spec_ref, left_scr, right_scr, vis_scr,
    in_sem, out_sem,
):
    n_inp, n_frq, n_loc, n_q, msg_rows, total_frames, rows_dev = cfg
    depth, inputs = spec_ref.shape
    per_lane = LANES // n_loc
    load = pltpu.make_async_copy(msg_hbm, msg_scr, in_sem)
    load.start()
    load.wait()

    row = lax.broadcasted_iota(jnp.int32, (msg_rows, LANES), 0)
    own = row < n_q
    later = (row >= n_q) & (row < 2 * n_q)
    lane_part = lax.broadcasted_iota(jnp.int32, (msg_rows, LANES), 1) // n_loc

    for m in range(n_inp // per_lane):
        msgs = [
            [
                msg_scr[((m * per_lane + e) * n_frq + f) * msg_rows :
                         ((m * per_lane + e) * n_frq + f + 1) * msg_rows, :]
                for e in range(per_lane)
            ]
            for f in range(n_frq)
        ]
        for c in range(per_lane):
            lined = []
            for f in range(n_frq):
                tile = None
                for e in range(per_lane):
                    turn = (e - c) * n_loc % LANES
                    piece = pltpu.roll(msgs[f][e], turn, 1) if turn else msgs[f][e]
                    tile = piece if tile is None else jnp.where(lane_part == e, piece, tile)
                lined.append(tile)
            for pair in range(n_frq // 2):
                even, odd = lined[2 * pair], lined[2 * pair + 1]
                total = even + jnp.where(later, pltpu.roll(odd, n_q, 0), 0.0)
                if pair:
                    before = pltpu.roll(lined[2 * pair - 1], msg_rows - n_q, 0)
                    total = total + jnp.where(own, before, 0.0)
                at = (pair * per_lane + c) * msg_rows
                spec_ref[at : at + msg_rows, m * LANES : (m + 1) * LANES] = total

    spectra = spec_ref[...]
    h, m, l = split_bf16(spectra, 3)
    spare = [jnp.zeros_like(h)] * (-6 % (LANES // depth) if LANES % depth == 0 else 0)
    right = jnp.concatenate([h, m, h, l, h, m] + spare, axis=0)
    anchor = pl.multiple_of(lax.axis_index("frq") * rows_dev, LANES)
    left = spec_ref[:, pl.ds(anchor, rows_dev)] * (1.0 / total_frames)
    row_at = lax.broadcasted_iota(jnp.int32, (msg_rows, rows_dev), 0)
    swapped = jnp.concatenate(
        [
            jnp.where(
                row_at % n_q < n_q // 2,
                pltpu.roll(left[at : at + msg_rows], msg_rows - n_q // 2, 0),
                -pltpu.roll(left[at : at + msg_rows], n_q // 2, 0),
            )
            for at in range(0, depth, msg_rows)
        ],
        axis=0,
    )
    h, m, l = split_bf16(jnp.concatenate([left, swapped], axis=1), 3)
    left_scr[...] = jnp.concatenate([h, h, m, h, l, m] + spare, axis=0).T
    right_scr[...] = right
    per_row = 2 * inputs // LANES
    copies = []
    for row, block in row_blocks(rows_dev):
        sides = [
            left_scr[part * rows_dev + row : part * rows_dev + row + block, :]
            for part in range(2)
        ]
        vis = jnp.dot(
            jnp.concatenate(sides, axis=0), right_scr[...], preferred_element_type=jnp.float32
        )
        for part in range(2):
            for r in range(0, block, SUBL):
                for tile in range(inputs // LANES):
                    at = (row + r) * per_row + 2 * tile + part
                    vis_scr[pl.ds(at, SUBL, stride=per_row), :] = vis[
                        part * block + r : part * block + r + SUBL,
                        tile * LANES : (tile + 1) * LANES,
                    ]
        rows = pl.ds(row * per_row, block * per_row)
        copies.append(
            pltpu.make_async_copy(vis_scr.at[rows], out_hbm.at[rows], out_sem.at[len(copies)])
        )
        copies[-1].start()
    for copy in copies:
        copy.wait()


def body(n_inp, n_frq, voltages, history, window):
    n_loc, frames, samples = voltages.shape
    taps = window.shape[0]
    inputs = n_loc * n_inp
    channels = CH_DEV * n_inp
    x = voltages.reshape(n_loc, frames, samples // LANES, LANES).transpose(0, 2, 1, 3)
    h = history.transpose(1, 0, 2).reshape((taps - 1) * n_loc, samples)
    table = jnp.asarray(dft_rows(channels, samples))

    per_lane = LANES // n_loc
    n_q = 2 * frames // per_lane
    msg_rows = -(-2 * n_q // SUBL) * SUBL
    depth = (n_frq // 2) * per_lane * msg_rows
    x_rows = n_loc * (frames + taps - 1)
    n_dev = n_inp * n_frq
    half = taps * 2 * channels
    spectra = pl.pallas_call(
        functools.partial(
            spectra_kernel, (n_inp, n_frq, n_loc, frames, taps, channels)
        ),
        out_shape=jax.ShapeDtypeStruct((n_dev * msg_rows, LANES), jnp.float32),
        in_specs=[pl.BlockSpec(memory_space=pl.ANY)] * 4,
        out_specs=pl.BlockSpec(memory_space=pl.ANY),
        scratch_shapes=[
            pltpu.VMEM((samples // LANES, n_loc, frames, LANES), jnp.bfloat16),
            pltpu.VMEM(((taps - 1) * n_loc, samples), jnp.bfloat16),
            pltpu.VMEM((2 * channels, samples), jnp.float32),
            pltpu.VMEM((taps, samples), jnp.float32),
            pltpu.VMEM((2 * half, samples), jnp.bfloat16),
            pltpu.VMEM((half // LANES, x_rows, LANES), jnp.float32),
            pltpu.VMEM((channels * msg_rows, LANES), jnp.float32),
            pltpu.SemaphoreType.DMA((4 + samples // LANES,)),
            pltpu.SemaphoreType.DMA,
            pltpu.SemaphoreType.DMA,
        ],
        compiler_params=pltpu.CompilerParams(
            collective_id=0, has_side_effects=True, vmem_limit_bytes=60 * 2**20
        ),
        name="spectra_exchange",
    )(x, h, table, window)

    rows_dev = inputs // n_frq
    stack = 6 * depth if LANES % depth else -(-6 * depth // LANES) * LANES
    per_row = 2 * inputs // LANES
    vis = pl.pallas_call(
        functools.partial(
            gram_kernel,
            (n_inp, n_frq, n_loc, n_q, msg_rows, frames * n_frq, rows_dev),
        ),
        out_shape=jax.ShapeDtypeStruct((rows_dev * per_row, LANES), jnp.float32),
        in_specs=[pl.BlockSpec(memory_space=pl.ANY)],
        out_specs=pl.BlockSpec(memory_space=pl.ANY),
        scratch_shapes=[
            pltpu.VMEM((n_dev * msg_rows, LANES), jnp.float32),
            pltpu.VMEM((depth, inputs), jnp.float32),
            pltpu.VMEM((2 * rows_dev, stack), jnp.bfloat16),
            pltpu.VMEM((stack, inputs), jnp.bfloat16),
            pltpu.VMEM((rows_dev * per_row, LANES), jnp.float32),
            pltpu.SemaphoreType.DMA,
            pltpu.SemaphoreType.DMA((len(row_blocks(rows_dev)),)),
        ],
        compiler_params=pltpu.CompilerParams(vmem_limit_bytes=60 * 2**20),
        name="gram",
    )(spectra)
    return (
        vis.reshape(rows_dev, inputs // LANES, 2, LANES)
        .transpose(0, 2, 1, 3)
        .reshape(rows_dev, 1, 2, inputs)
    )


def solution(mesh):
    return jax.shard_map(
        functools.partial(body, mesh.shape["inp"], mesh.shape["frq"]),
        mesh=mesh,
        in_specs=(P("inp", "frq", None), P("inp", None, None), P()),
        out_specs=P("frq", "inp", None, None),
        check_vma=False,
    )
```

```python
import functools
import math

import jax
import jax.numpy as jnp
import numpy as np
from jax import lax
from jax.experimental import pallas as pl
from jax.experimental.pallas import tpu as pltpu
from jax.sharding import PartitionSpec as P

CH_DEV = 1
LANES = 128
SUBL = 8
MESH = pl.DeviceIdType.MESH


def dft_rows(channels, samples):
    first_bin = (samples // 2 - channels) // 2
    bins = np.arange(channels, dtype=np.int64) + first_bin
    turns = bins[:, None] * np.arange(samples, dtype=np.int64)[None, :] % samples
    phases = turns * (2.0 * math.pi / samples)
    table = np.concatenate([np.cos(phases), -np.sin(phases)], axis=0) / math.sqrt(samples)
    return table.astype(np.float32)


def split_bf16(value, pieces):
    out = []
    for _ in range(pieces):
        piece = value.astype(jnp.bfloat16)
        out.append(piece)
        value = value - piece.astype(jnp.float32)
    return out


def to_others(n_inp, n_frq, my_inp, my_frq, act):
    def group(ahead, low):
        to_inp = lax.rem(my_inp + ahead, n_inp)
        for turn in range(low, n_frq):
            act(to_inp, lax.rem(my_frq + turn, n_frq))

    if n_inp * n_frq <= 32:
        for step in range(n_inp - 1):
            group((n_inp // 2 + step) % n_inp if step < n_inp // 2 else n_inp - 1 - step, 0)
    else:
        lax.fori_loop(1, n_inp, lambda step, carry: (group(step, 0), carry)[1], 0)
    group(0, 1)


def spectra_kernel(
    cfg, x_hbm, h_hbm, table_hbm, window_hbm, out_hbm,
    x_scr, h_scr, table_scr, window_scr, mat_scr, z_scr, msg_scr,
    in_sem, send_sem, recv_sem,
):
    n_inp, n_frq, n_loc, frames, taps, channels = cfg
    n_dev = n_inp * n_frq
    my_inp = lax.axis_index("inp")
    my_frq = lax.axis_index("frq")
    me = my_inp * n_frq + my_frq
    v_rows = n_loc * frames
    loads = [
        pltpu.make_async_copy(table_hbm, table_scr, in_sem.at[0]),
        pltpu.make_async_copy(window_hbm, window_scr, in_sem.at[1]),
        pltpu.make_async_copy(h_hbm, h_scr, in_sem.at[2]),
        pltpu.make_async_copy(x_hbm, x_scr, in_sem.at[3]),
    ]
    for load in loads:
        load.start()

    barrier = pltpu.get_barrier_semaphore()

    def greet(to_inp, to_frq):
        pl.semaphore_signal(barrier, inc=1, device_id=(to_inp, to_frq), device_id_type=MESH)

    to_others(n_inp, n_frq, my_inp, my_frq, greet)

    loads[0].wait()
    loads[1].wait()
    group = 2 * channels
    for tap in range(taps):
        hi, lo = split_bf16(window_scr[tap : tap + 1, :] * table_scr[...], 2)
        mat_scr[tap * group : (tap + 1) * group, :] = hi
        mat_scr[(taps + tap) * group : (taps + tap + 1) * group, :] = lo
    half = taps * group
    tiles = half // LANES

    loads[2].wait()
    loads[3].wait()
    rows = jnp.concatenate([x_scr[...].reshape(v_rows, x_scr.shape[2]), h_scr[...]], axis=0)
    z = lax.dot_general(
        rows, mat_scr[...], (((1,), (1,)), ((), ())), preferred_element_type=jnp.float32
    )
    for tile in range(tiles):
        z_scr[tile] = (
            z[:, tile * LANES : (tile + 1) * LANES]
            + z[:, half + tile * LANES : half + (tile + 1) * LANES]
        )

    first = my_frq == 0

    def frame(tile, u):
        if u >= frames:
            return None
        if u >= 0:
            return z_scr[tile, pl.ds(u, n_loc, stride=frames), :]
        at = v_rows + (u + taps - 1) * n_loc
        rows = z_scr[tile, at : at + n_loc, :]
        return jnp.where(first, rows, 0.0)

    held = {(tile, u): frame(tile, u) for tile in range(tiles) for u in range(1 - taps, frames)}
    per_tile = LANES // group
    lane_group = lax.broadcasted_iota(jnp.int32, (n_loc, LANES), 1) // group
    per_lane = LANES // n_loc
    n_q = 2 * frames // per_lane
    half_q = n_q // 2
    msg_rows = msg_scr.shape[0] // channels

    def frame_products(tile, t):
        total = jnp.zeros((n_loc, LANES), jnp.float32)
        for g in range(per_tile):
            u = t - (taps - 1) + tile * per_tile + g
            part = held.get((tile, u))
            if part is not None:
                total = jnp.where(lane_group == g, part, total)
        return total

    for q in range(n_q):
        acc = None
        for tile in range(tiles):
            block = jnp.concatenate(
                [frame_products(tile, q * per_lane + c) for c in range(per_lane)], axis=0
            ).T
            for g in range(per_tile):
                part = block[g * group : (g + 1) * group]
                acc = part if acc is None else acc + part
        for part in range(2):
            for jb in range(channels // SUBL):
                row = part * channels + jb * SUBL
                at = q // half_q * n_q + part * half_q + q % half_q
                msg_scr[pl.ds(jb * SUBL * msg_rows + at, SUBL, stride=msg_rows), :] = acc[
                    row : row + SUBL
                ]
    if msg_rows > 2 * n_q:
        for row in range(2 * n_q, msg_rows):
            for jb in range(channels // SUBL):
                msg_scr[pl.ds(jb * SUBL * msg_rows + row, SUBL, stride=msg_rows), :] = jnp.zeros(
                    (SUBL, LANES), jnp.float32
                )

    own_rows = n_q if n_q % 4 == 0 else msg_rows

    def exchange(rows, waited):
        my_slot = out_hbm.at[pl.ds(pl.multiple_of(me * msg_rows, SUBL), rows)]

        def message(to_inp):
            return msg_scr.at[pl.ds(pl.multiple_of(to_inp * msg_rows, SUBL), rows)]

        def send(to_inp, to_frq):
            pltpu.make_async_remote_copy(
                src_ref=message(to_inp),
                dst_ref=my_slot,
                send_sem=send_sem,
                recv_sem=recv_sem,
                device_id=(to_inp, to_frq),
                device_id_type=MESH,
            ).start()

        def bytes_of(count):
            return pltpu.make_async_remote_copy(
                src_ref=out_hbm.at[pl.ds(0, count)],
                dst_ref=out_hbm.at[pl.ds(0, count)],
                send_sem=send_sem,
                recv_sem=recv_sem,
                device_id=(my_inp, my_frq),
                device_id_type=MESH,
            )

        mine = pltpu.make_async_copy(message(my_inp), my_slot, in_sem.at[4])
        mine.start()
        to_others(n_inp, n_frq, my_inp, my_frq, send)
        bytes_of(waited).wait_recv()
        bytes_of((n_dev - 1) * rows).wait_send()
        mine.wait()

    pl.semaphore_wait(barrier, n_dev - 1)
    arriving = n_inp * ((n_frq - 1) * msg_rows + own_rows)
    last = my_frq == n_frq - 1
    pl.when(last)(lambda: exchange(own_rows, arriving - own_rows))
    pl.when(jnp.logical_not(last))(lambda: exchange(msg_rows, arriving - msg_rows))


def gram_kernel(
    cfg, msg_hbm, out_hbm, msg_scr, spec_ref, left_scr, right_scr, vis_scr,
    in_sem, out_sem,
):
    n_inp, n_frq, n_loc, n_q, msg_rows, total_frames, rows_dev = cfg
    depth, inputs = spec_ref.shape
    per_lane = LANES // n_loc
    load = pltpu.make_async_copy(msg_hbm, msg_scr, in_sem)
    load.start()
    load.wait()

    row = lax.broadcasted_iota(jnp.int32, (msg_rows, LANES), 0)
    own = row < n_q
    later = (row >= n_q) & (row < 2 * n_q)
    lane_part = lax.broadcasted_iota(jnp.int32, (msg_rows, LANES), 1) // n_loc

    for m in range(n_inp // per_lane):
        msgs = [
            [
                msg_scr[((m * per_lane + e) * n_frq + f) * msg_rows :
                         ((m * per_lane + e) * n_frq + f + 1) * msg_rows, :]
                for e in range(per_lane)
            ]
            for f in range(n_frq)
        ]
        for c in range(per_lane):
            lined = []
            for f in range(n_frq):
                tile = None
                for e in range(per_lane):
                    turn = (e - c) * n_loc % LANES
                    piece = pltpu.roll(msgs[f][e], turn, 1) if turn else msgs[f][e]
                    tile = piece if tile is None else jnp.where(lane_part == e, piece, tile)
                lined.append(tile)
            for pair in range(n_frq // 2):
                even, odd = lined[2 * pair], lined[2 * pair + 1]
                total = even + jnp.where(later, pltpu.roll(odd, n_q, 0), 0.0)
                if pair:
                    before = pltpu.roll(lined[2 * pair - 1], msg_rows - n_q, 0)
                    total = total + jnp.where(own, before, 0.0)
                at = (pair * per_lane + c) * msg_rows
                spec_ref[at : at + msg_rows, m * LANES : (m + 1) * LANES] = total

    spectra = spec_ref[...]
    h, m, l = split_bf16(spectra, 3)
    spare = [jnp.zeros_like(h)] * (-6 % (LANES // depth) if LANES % depth == 0 else 0)
    right = jnp.concatenate([h, m, h, l, h, m] + spare, axis=0)
    anchor = pl.multiple_of(lax.axis_index("frq") * rows_dev, LANES)
    left = spec_ref[:, pl.ds(anchor, rows_dev)] * (1.0 / total_frames)
    row_at = lax.broadcasted_iota(jnp.int32, (msg_rows, rows_dev), 0)
    swapped = jnp.concatenate(
        [
            jnp.where(
                row_at % n_q < n_q // 2,
                pltpu.roll(left[at : at + msg_rows], msg_rows - n_q // 2, 0),
                -pltpu.roll(left[at : at + msg_rows], n_q // 2, 0),
            )
            for at in range(0, depth, msg_rows)
        ],
        axis=0,
    )
    h, m, l = split_bf16(jnp.concatenate([left, swapped], axis=1), 3)
    left_scr[...] = jnp.concatenate([h, h, m, h, l, m] + spare, axis=0).T
    right_scr[...] = right
    width = 2 * LANES
    copies = []
    for block in range(inputs // width):
        vis = jnp.dot(
            left_scr[...],
            right_scr[:, block * width : (block + 1) * width],
            preferred_element_type=jnp.float32,
        )
        for tile in range(2):
            for part in range(2):
                at = 2 * (2 * block + tile) + part
                vis_scr[at] = vis[
                    part * rows_dev : (part + 1) * rows_dev, tile * LANES : (tile + 1) * LANES
                ]
                copy = pltpu.make_async_copy(vis_scr.at[at], out_hbm.at[:, at], out_sem.at[at])
                copy.start()
                copies.append(copy)
    for copy in copies:
        copy.wait()


def body(n_inp, n_frq, voltages, history, window):
    n_loc, frames, samples = voltages.shape
    taps = window.shape[0]
    inputs = n_loc * n_inp
    channels = CH_DEV * n_inp
    h = history.transpose(1, 0, 2).reshape((taps - 1) * n_loc, samples)
    table = jnp.asarray(dft_rows(channels, samples))

    per_lane = LANES // n_loc
    n_q = 2 * frames // per_lane
    msg_rows = -(-2 * n_q // SUBL) * SUBL
    depth = (n_frq // 2) * per_lane * msg_rows
    x_rows = n_loc * (frames + taps - 1)
    n_dev = n_inp * n_frq
    half = taps * 2 * channels
    spectra = pl.pallas_call(
        functools.partial(
            spectra_kernel, (n_inp, n_frq, n_loc, frames, taps, channels)
        ),
        out_shape=jax.ShapeDtypeStruct((n_dev * msg_rows, LANES), jnp.float32),
        in_specs=[pl.BlockSpec(memory_space=pl.ANY)] * 4,
        out_specs=pl.BlockSpec(memory_space=pl.ANY),
        scratch_shapes=[
            pltpu.VMEM((n_loc, frames, samples), jnp.bfloat16),
            pltpu.VMEM(((taps - 1) * n_loc, samples), jnp.bfloat16),
            pltpu.VMEM((2 * channels, samples), jnp.float32),
            pltpu.VMEM((taps, samples), jnp.float32),
            pltpu.VMEM((2 * half, samples), jnp.bfloat16),
            pltpu.VMEM((half // LANES, x_rows, LANES), jnp.float32),
            pltpu.VMEM((channels * msg_rows, LANES), jnp.float32),
            pltpu.SemaphoreType.DMA((5,)),
            pltpu.SemaphoreType.DMA,
            pltpu.SemaphoreType.DMA,
        ],
        compiler_params=pltpu.CompilerParams(
            collective_id=0, has_side_effects=True, vmem_limit_bytes=60 * 2**20
        ),
        name="spectra_exchange",
    )(voltages, h, table, window)

    rows_dev = inputs // n_frq
    stack = 6 * depth if LANES % depth else -(-6 * depth // LANES) * LANES
    per_row = 2 * inputs // LANES
    vis = pl.pallas_call(
        functools.partial(
            gram_kernel,
            (n_inp, n_frq, n_loc, n_q, msg_rows, frames * n_frq, rows_dev),
        ),
        out_shape=jax.ShapeDtypeStruct((rows_dev, per_row, LANES), jnp.float32),
        in_specs=[pl.BlockSpec(memory_space=pl.ANY)],
        out_specs=pl.BlockSpec(memory_space=pl.ANY),
        scratch_shapes=[
            pltpu.VMEM((n_dev * msg_rows, LANES), jnp.float32),
            pltpu.VMEM((depth, inputs), jnp.float32),
            pltpu.VMEM((2 * rows_dev, stack), jnp.bfloat16),
            pltpu.VMEM((stack, inputs), jnp.bfloat16),
            pltpu.VMEM((per_row, rows_dev, LANES), jnp.float32),
            pltpu.SemaphoreType.DMA,
            pltpu.SemaphoreType.DMA((per_row,)),
        ],
        compiler_params=pltpu.CompilerParams(vmem_limit_bytes=60 * 2**20),
        name="gram",
    )(spectra)
    return (
        vis.reshape(rows_dev, inputs // LANES, 2, LANES)
        .transpose(0, 2, 1, 3)
        .reshape(rows_dev, 1, 2, inputs)
    )


def solution(mesh):
    return jax.shard_map(
        functools.partial(body, mesh.shape["inp"], mesh.shape["frq"]),
        mesh=mesh,
        in_specs=(P("inp", "frq", None), P("inp", None, None), P()),
        out_specs=P("frq", "inp", None, None),
        check_vma=False,
    )
```
